128 devices in a mesh: lat: 4 (over z_hi, core), lon: 32 (over x, y, z_lo).
Axes of the slice: x: 4, y: 4, z: 4 (z_hi: 2, z_lo: 2; z = z_hi * 2 + z_lo), core: 2. Of those that a mesh axis runs over, the one named last changes fastest.
Arguments:
- pixels: bfloat16 [4, 24, 768, 500], P(None, 'lat', 'lon'), may hold values from -6 to 6
- land_patch_mask: int32 [24, 768], P('lat', 'lon'), may hold values 0 or 1
- region: int32 [2, 4, 64], P(None, 'lat', 'lon'), may hold values from 0 to 31
- patch_embed_weight: bfloat16 [500, 512], replicated, may hold values from -0.25 to 0.25
- patch_embed_bias: float32 [512], replicated, may hold values from -4 to 4
- land_embedding_vector: float32 [512], replicated, may hold values from -4 to 4
- attention_norm_gain: float32 [512], replicated, may hold values from 0.1 to 1.9
- query_key_value_weight: bfloat16 [512, 1536], replicated, may hold values from -0.25 to 0.25
- region_down_factor: bfloat16 [32, 8, 512], replicated, may hold values from -0.25 to 0.25
- region_up_factor: bfloat16 [32, 8, 1536], replicated, may hold values from -2 to 2
- head_logit_scale: float32 [16], replicated, may hold values from 1 to 10
- attention_output_weight: bfloat16 [512, 512], replicated, may hold values from -0.25 to 0.25
- feedforward_gain: float32 [512], replicated, may hold values from 0.1 to 1.9
- feedforward_up_weight: bfloat16 [512, 2048], replicated, may hold values from -0.25 to 0.25
- feedforward_down_weight: bfloat16 [2048, 512], replicated, may hold values from -0.125 to 0.125
- cotangent: float32 [4, 24, 768, 512], P(None, 'lat', 'lon'), may hold values from -6 to 6
Outputs:
- mixed_state: float32 [4, 24, 768, 512], P(None, 'lat', 'lon')
- step_down: float32 [32, 8, 512], replicated
- step_up: float32 [32, 8, 1536], replicated
The draws below stay inside these ranges and needn't reach their ends.
All inputs are finite; a program needn't handle non-finite values. No bound on the sum of `land_patch_mask` on one device may be relied on, other than what follows from the above.
Results may differ from the reference program's by a relative error of at most 0.015.
Values may be sent and summed in bfloat16 or wider, within the bound.
No kernel may reach another device: no remote copies, remote signals or barrier semaphores. Data moves between devices by JAX's collectives and lax.ppermute only.
A program may use at most 128 MiB of HBM per device.

```python
import math
import jax
import jax.numpy as jnp
from jax import lax

HEADS = 16
MODEL_WIDTH = 512
FF = 2048
PATCH_LEN = 500
ADAPTER_RANK = 8
REGION_COUNT = 32
LEV = 4
WLEV = 2
WLAT = 6
WLON = 12
NLAT = 24
NLON = 768


def set_ends(drawn, own_key, smallest, high):
    shape = drawn.shape
    index_at = [jax.random.randint(jax.random.fold_in(own_key, axis), (), 0, shape[axis]) for axis in range(len(shape))]
    drawn = drawn.at[tuple(index_at)].set(smallest)
    longest = shape.index(max(shape))
    index_at[longest] = (index_at[longest] + 1) % shape[longest]
    return drawn.at[tuple(index_at)].set(high)


def block_levels(own_key, dims, cuts, low, largest):
    factor_of, own = 1.0, jax.random.fold_in(own_key, 6)
    for position, blocks in cuts:
        heights = jnp.exp(jax.random.uniform(jax.random.fold_in(own, position), (blocks,), jnp.float32, low / len(cuts), largest / len(cuts)))
        factor_of = factor_of * jnp.repeat(heights, dims[position] // blocks).reshape([-1 if axis == position else 1 for axis in range(len(dims))])
    return factor_of


def gaussian(stream_key, extent, scale, reach, cuts=(), held_as=jnp.bfloat16):
    drawn = jax.random.normal(stream_key, extent, jnp.float32) * scale
    if len(cuts) > 0:
        drawn = block_levels(stream_key, extent, cuts, -0.22, 0.18) * drawn
    return jnp.clip(drawn, min=-reach, max=reach).astype(held_as)


def setup_inputs(seed: int = 0) -> dict:
    splits = jax.random.split(jax.random.key(seed), 17)
    pixels = gaussian(splits[0], (LEV, NLAT, NLON, PATCH_LEN), 1.0, 6.0, ((1, 4), (2, 32)))
    land_patch_mask = set_ends((jax.random.randint(splits[1], (NLAT, NLON), 0, 3) < 1).astype(jnp.int32), jax.random.fold_in(splits[1], 1), 0, 1)
    region = set_ends(jax.random.randint(splits[2], (LEV // WLEV, NLAT // WLAT, NLON // WLON), 0, REGION_COUNT), jax.random.fold_in(splits[2], 1), 0, REGION_COUNT - 1).astype(jnp.int32)
    patch_embed_weight = gaussian(splits[3], (PATCH_LEN, MODEL_WIDTH), PATCH_LEN ** -0.5, 0.25)
    patch_embed_bias = gaussian(splits[4], (MODEL_WIDTH,), 1.0, 4.0, (), jnp.float32)
    land_embedding_vector = gaussian(splits[5], (MODEL_WIDTH,), 1.0, 4.0, (), jnp.float32)
    attention_norm_gain = jnp.clip(1.0 + 0.18 * jax.random.normal(splits[6], (MODEL_WIDTH,), jnp.float32), 0.1, 1.9)
    query_key_value_weight = gaussian(splits[7], (MODEL_WIDTH, 3 * MODEL_WIDTH), MODEL_WIDTH ** -0.5, 0.25)
    region_down_factor = gaussian(splits[8], (REGION_COUNT, ADAPTER_RANK, MODEL_WIDTH), MODEL_WIDTH ** -0.5, 0.25)
    region_up_factor = gaussian(splits[9], (REGION_COUNT, ADAPTER_RANK, 3 * MODEL_WIDTH), ADAPTER_RANK ** -0.5, 2.0)
    head_logit_scale = jnp.clip(jnp.exp(jax.random.uniform(splits[10], (HEADS,), jnp.float32, math.log(1.0), math.log(10.0))), 1.0, 10.0)
    attention_output_weight = gaussian(splits[11], (MODEL_WIDTH, MODEL_WIDTH), MODEL_WIDTH ** -0.5, 0.25)
    feedforward_gain = jnp.clip(1.0 + 0.18 * jax.random.normal(splits[12], (MODEL_WIDTH,), jnp.float32), 0.1, 1.9)
    feedforward_up_weight = gaussian(splits[13], (MODEL_WIDTH, FF), MODEL_WIDTH ** -0.5, 0.25)
    feedforward_down_weight = gaussian(splits[14], (FF, MODEL_WIDTH), FF ** -0.5, 0.125)
    cotangent = gaussian(splits[15], (LEV, NLAT, NLON, MODEL_WIDTH), 1.0, 6.0, ((1, 4), (2, 32)), jnp.float32)
    return {"pixels": pixels, "land_patch_mask": land_patch_mask, "region": region, "patch_embed_weight": patch_embed_weight, "patch_embed_bias": patch_embed_bias, "land_embedding_vector": land_embedding_vector, "attention_norm_gain": attention_norm_gain, "query_key_value_weight": query_key_value_weight, "region_down_factor": region_down_factor, "region_up_factor": region_up_factor, "head_logit_scale": head_logit_scale, "attention_output_weight": attention_output_weight, "feedforward_gain": feedforward_gain, "feedforward_up_weight": feedforward_up_weight, "feedforward_down_weight": feedforward_down_weight, "cotangent": cotangent}


HIGH = lax.Precision.HIGHEST

def layer_norm(field, gain):
    mean = lax.optimization_barrier(jnp.mean(field, axis=-1, keepdims=True))
    centred = field - mean
    spread = lax.optimization_barrier(jnp.mean(centred * centred, axis=-1, keepdims=True))
    return (centred * lax.rsqrt(spread + 1e-05) * gain).astype(jnp.bfloat16)

def embed(pixels, land_patch_mask, patch_embed_weight, patch_embed_bias, land_embedding_vector):
    levels, rows, cols, patch_len = pixels.shape
    flat = jnp.dot(pixels.reshape(-1, patch_len), patch_embed_weight, preferred_element_type=jnp.float32)
    land = land_patch_mask.astype(jnp.float32)[None, :, :, None] * land_embedding_vector
    return flat.reshape(levels, rows, cols, -1) + patch_embed_bias + land

def to_windows(field):
    levels, rows, cols, width = field.shape
    field = field.reshape(levels // WLEV, WLEV, rows // WLAT, WLAT, cols // WLON, WLON, width)
    field = field.transpose(0, 2, 4, 1, 3, 5, 6)
    return field.reshape(-1, WLEV * WLAT * WLON, width)

def from_windows(window_tokens, levels, rows, cols):
    width = window_tokens.shape[-1]
    field = window_tokens.reshape(levels // WLEV, rows // WLAT, cols // WLON, WLEV, WLAT, WLON, width)
    field = field.transpose(0, 3, 1, 4, 2, 5, 6)
    return field.reshape(levels, rows, cols, width)

def apply_projection(window_tokens, region_index, query_key_value_weight, region_down_factor, region_up_factor):
    count, tokens, width = window_tokens.shape
    base = jnp.dot(window_tokens.reshape(-1, width), query_key_value_weight, preferred_element_type=jnp.float32)
    down_factor = jnp.take(region_down_factor, region_index, axis=0).astype(jnp.float32)
    upper_bound = jnp.take(region_up_factor, region_index, axis=0).astype(jnp.float32)
    low_rank_state = jnp.einsum('wtd,wrd->wtr', window_tokens.astype(jnp.float32), down_factor, precision=HIGH).astype(jnp.bfloat16)
    extra = jnp.einsum('wtr,wrc->wtc', low_rank_state.astype(jnp.float32), upper_bound, precision=HIGH)
    return (base.reshape(count, tokens, -1) + extra, low_rank_state)

def attend(query_key_value, groups, head_logit_scale, attention_output_weight):
    count, tokens, triple = query_key_value.shape
    heads = head_logit_scale.shape[0]
    size = triple // (3 * heads)
    parts = query_key_value.reshape(count, tokens, 3, heads, size)
    query = parts[:, :, 0]
    key = parts[:, :, 1]
    value = parts[:, :, 2].astype(jnp.bfloat16).astype(jnp.float32)
    query = query * lax.rsqrt(lax.optimization_barrier(jnp.mean(query * query, axis=-1, keepdims=True)) + 1e-06)
    key = key * lax.rsqrt(lax.optimization_barrier(jnp.mean(key * key, axis=-1, keepdims=True)) + 1e-06)
    scores = jnp.einsum('wqhe,wkhe->whqk', query, key, precision=HIGH)
    scores = scores * (head_logit_scale / size)[None, :, None, None]
    same = (groups[:, :, None] == groups[:, None, :])[:, None]
    weights = jnp.where(same, jnp.exp(scores), 0.0)
    probs = (weights / lax.optimization_barrier(jnp.sum(weights, axis=-1, keepdims=True))).astype(jnp.bfloat16)
    mixed = jnp.einsum('whqk,wkhe->wqhe', probs.astype(jnp.float32), value, precision=HIGH)
    mixed = mixed.reshape(count * tokens, heads * size).astype(jnp.bfloat16)
    out = jnp.dot(mixed, attention_output_weight, preferred_element_type=jnp.float32).astype(jnp.bfloat16)
    return out.reshape(count, tokens, -1)

def adapter_pieces(window_tokens, low_rank_state, grad_query_key_value, region_index, region_up_factor):
    total_sum = region_up_factor.shape[0]
    upper_bound = jnp.take(region_up_factor, region_index, axis=0).astype(jnp.float32)
    grad_up = jnp.einsum('wtr,wtc->wrc', low_rank_state.astype(jnp.float32), grad_query_key_value, precision=HIGH)
    back = jnp.einsum('wtc,wrc->wtr', grad_query_key_value, upper_bound, precision=HIGH)
    grad_down = jnp.einsum('wtr,wtd->wrd', back, window_tokens.astype(jnp.float32), precision=HIGH)
    onehot = (region_index[:, None] == jnp.arange(total_sum, dtype=jnp.int32)[None, :]).astype(jnp.float32)
    sum_down = jnp.einsum('wg,wrd->grd', onehot, grad_down, precision=HIGH)
    sum_up = jnp.einsum('wg,wrc->grc', onehot, grad_up, precision=HIGH)
    return (sum_down, sum_up)

def feed(state, gain, feedforward_up_weight, feedforward_down_weight):
    array_shape = state.shape
    normed = layer_norm(state, gain).reshape(-1, array_shape[-1])
    inner = jax.nn.gelu(jnp.dot(normed, feedforward_up_weight, preferred_element_type=jnp.float32), approximate=False)
    inner = inner.astype(jnp.bfloat16)
    return state + jnp.dot(inner, feedforward_down_weight, preferred_element_type=jnp.float32).reshape(array_shape)

def reference(pixels, land_patch_mask, region, patch_embed_weight, patch_embed_bias, land_embedding_vector, attention_norm_gain, query_key_value_weight, region_down_factor, region_up_factor, head_logit_scale, attention_output_weight, feedforward_gain, feedforward_up_weight, feedforward_down_weight, cotangent):
    state = embed(pixels, land_patch_mask, patch_embed_weight, patch_embed_bias, land_embedding_vector)
    normed = layer_norm(state, attention_norm_gain)
    forward_shift = (-(WLEV // 2), -(WLAT // 2), -(WLON // 2))
    backward_shift = (WLEV // 2, WLAT // 2, WLON // 2)
    rolled = jnp.roll(normed, forward_shift, axis=(0, 1, 2))
    level_flag = (jnp.arange(LEV) == LEV - 1).astype(jnp.int32)
    lat_flag = (jnp.arange(NLAT) >= NLAT - WLAT // 2).astype(jnp.int32)
    groups = jnp.broadcast_to(level_flag[:, None, None] * 2 + lat_flag[None, :, None], (LEV, NLAT, NLON))
    group_win = to_windows(groups[..., None])[..., 0]
    window_tokens = to_windows(rolled)
    tokens = WLEV * WLAT * WLON
    per_block = NLON // WLON
    blocks = window_tokens.shape[0] // per_block
    win_blocks = window_tokens.reshape(blocks, per_block, tokens, MODEL_WIDTH)
    reg_blocks = region.reshape(blocks, per_block)
    grp_blocks = group_win.reshape(blocks, per_block, tokens)

    def forward_block(item):
        visited_regions, region_index, marks = item
        query_key_value, low_rank_state = apply_projection(visited_regions, region_index, query_key_value_weight, region_down_factor, region_up_factor)
        return attend(query_key_value, marks, head_logit_scale, attention_output_weight)
    z_win = lax.map(forward_block, (win_blocks, reg_blocks, grp_blocks)).reshape(-1, tokens, MODEL_WIDTH)
    z_field = from_windows(z_win, LEV, NLAT, NLON)
    hidden = state + jnp.roll(z_field, backward_shift, axis=(0, 1, 2)).astype(jnp.float32)

    def mlp_block(item):
        rows_now, grad_now = item
        result, pull = jax.vjp(lambda v: feed(v, feedforward_gain, feedforward_up_weight, feedforward_down_weight), rows_now)
        return (result, pull(grad_now)[0])
    outs, grads = lax.map(mlp_block, (hidden.reshape(-1, NLON, MODEL_WIDTH), cotangent.reshape(-1, NLON, MODEL_WIDTH)))
    mixed_state = outs.reshape(LEV, NLAT, NLON, MODEL_WIDTH)
    d_hidden = grads.reshape(LEV, NLAT, NLON, MODEL_WIDTH).astype(jnp.bfloat16)
    d_win = to_windows(jnp.roll(d_hidden, forward_shift, axis=(0, 1, 2))).reshape(blocks, per_block, tokens, MODEL_WIDTH)

    def backward_block(item):
        visited_regions, region_index, marks, d_out = item
        query_key_value, low_rank_state = apply_projection(visited_regions, region_index, query_key_value_weight, region_down_factor, region_up_factor)
        unused, pull = jax.vjp(lambda q: attend(q, marks, head_logit_scale, attention_output_weight), query_key_value)
        grad_query_key_value = pull(d_out)[0]
        return adapter_pieces(visited_regions, low_rank_state, grad_query_key_value, region_index, region_up_factor)
    partial_down_grad, partial_up_grad = lax.map(backward_block, (win_blocks, reg_blocks, grp_blocks, d_win))
    grad_down = lax.optimization_barrier(jnp.sum(partial_down_grad, axis=0))
    grad_up = lax.optimization_barrier(jnp.sum(partial_up_grad, axis=0))
    squares = jnp.sum(grad_down * grad_down) + jnp.sum(grad_up * grad_up)
    factor = lax.rsqrt(squares / (grad_down.size + grad_up.size) + 1e-06)
    return (mixed_state, grad_down * factor, grad_up * factor)
```

```python
import jax
import jax.numpy as jnp
from jax import lax
from jax.experimental import pallas as pl
from jax.experimental.pallas import tpu as pltpu
from jax.sharding import PartitionSpec as P

WLEV = 2
WLAT = 6
WLON = 12
TOKENS = WLEV * WLAT * WLON
HALF_LAT = WLAT // 2
HALF_LON = WLON // 2
LANES = 128
HEAD = 32
PER_GROUP = LANES // HEAD

F32 = jnp.float32
BF16 = jnp.bfloat16
VMEM_LIMIT = 56 * 1024 * 1024


def mm(a, b):
    return lax.dot_general(a, b, (((1,), (0,)), ((), ())), preferred_element_type=F32)


def mm_nt(a, b):
    return lax.dot_general(a, b, (((1,), (1,)), ((), ())), preferred_element_type=F32)


def mm_tn(a, b):
    return lax.dot_general(a, b, (((0,), (0,)), ((), ())), preferred_element_type=F32)


def head_mean(squares):
    rows = lax.broadcasted_iota(jnp.int32, (LANES, LANES), 0) // HEAD
    cols = lax.broadcasted_iota(jnp.int32, (LANES, LANES), 1) // HEAD
    block = jnp.where(rows == cols, 1.0 / HEAD, 0.0).astype(BF16)
    parts = []
    for g in range(squares.shape[1] // LANES):
        part = squares[:, g * LANES : (g + 1) * LANES]
        top = part.astype(BF16)
        rest = (part - top.astype(F32)).astype(BF16)
        parts.append(mm(top, block) + mm(rest, block))
    return jnp.concatenate(parts, axis=1)


def head_masks():
    lane = lax.broadcasted_iota(jnp.int32, (1, LANES), 1) // HEAD
    return [jnp.where(lane == h, 1.0, 0.0).astype(F32) for h in range(PER_GROUP)]


def stack_heads(x, masks):
    return jnp.concatenate([(x * m).astype(BF16) for m in masks], axis=0)


def unstack_heads(x, masks):
    tokens = x.shape[0] // PER_GROUP
    return sum(x[h * tokens : (h + 1) * tokens] * m for h, m in enumerate(masks))


def window_columns(tokens, columns):
    count = tokens // TOKENS
    rows = lax.broadcasted_iota(jnp.int32, (tokens, columns), 0)
    cols = lax.broadcasted_iota(jnp.int32, (tokens, columns), 1) % count
    own = jnp.zeros((tokens, columns), F32)
    for w in range(count):
        inside = (rows >= w * TOKENS) & (rows < (w + 1) * TOKENS) & (cols == w)
        own = jnp.where(inside, 1.0, own)
    return own


def norm_stats(x):
    width = x.shape[1]
    mean = jnp.sum(x, axis=1, keepdims=True) * (1.0 / width)
    centred = x - mean
    spread = jnp.sum(centred * centred, axis=1, keepdims=True) * (1.0 / width)
    return centred, lax.rsqrt(spread + 1e-05)


def gelu_and_slope(u):
    x = jnp.abs(u) * 0.7071067811865476
    t = 1.0 / (1.0 + 0.3275911 * x)
    e = jnp.exp(-0.5 * u * u)
    poly = 1.061405429
    for c in (-1.453152027, 1.421413741, -0.284496736, 0.254829592):
        poly = poly * t + c
    tail = 0.5 * poly * t * e
    phi = jnp.where(u < 0, tail, 1.0 - tail)
    return u * phi, phi + u * (0.3989422804014327 * e)


def forward_kernel(
    pix_ref, wp_ref, bias_ref, land_ref, gain1_ref, wqkv_ref, down_ref, up_ref, scale_ref,
    same_ref, wo_ref, gain2_ref, wup_ref, wdn_ref, cot_ref,
    mixed_ref, normed_ref, low_ref, qk_ref, v_ref, probs_ref, datt_ref,
    state_ref, qs_ref, kn_ref, att_ref,
):
    tokens, width = state_ref.shape
    count = tokens // TOKENS
    groups = width // LANES
    masks = head_masks()
    pix = pix_ref[...]
    patch_len = wp_ref.shape[0]
    land = pix[:, 500:501].astype(F32)
    state = mm(pix, wp_ref[...]) + bias_ref[...] + land * land_ref[...]
    state_ref[...] = state
    centred, inv = norm_stats(state)
    normed = (centred * inv * gain1_ref[...]).astype(BF16)
    normed_ref[...] = normed
    low = (mm_nt(normed, down_ref[...]) * window_columns(tokens, down_ref.shape[0])).astype(BF16)
    low_ref[...] = low
    for part in range(3):
        cols = slice(part * width, (part + 1) * width)
        qkv = mm(normed, wqkv_ref[:, cols]) + mm(low, up_ref[:, cols])
        if part == 2:
            v_ref[...] = qkv.astype(BF16)
        else:
            qk_ref[:, cols] = qkv
            unit = qkv * lax.rsqrt(head_mean(qkv * qkv) + 1e-06)
            if part == 0:
                qs_ref[...] = unit * scale_ref[...]
            else:
                kn_ref[...] = unit.astype(BF16)

    def window(w, carry):
        rows = pl.ds(pl.multiple_of(w * TOKENS, TOKENS), TOKENS)
        same = same_ref[w // (count // WLEV)]
        for g in range(groups):
            cols = slice(g * LANES, (g + 1) * LANES)
            stack = stack_heads(qs_ref[rows, cols], masks)
            weights = jnp.exp(mm_nt(kn_ref[rows, cols], stack)) * same
            total = jnp.sum(weights, axis=0, keepdims=True)
            probs = (weights * (1.0 / total)).astype(BF16)
            probs_ref[w * groups + g] = probs
            mixed = mm_tn(probs, v_ref[rows, cols])
            att_ref[rows, cols] = unstack_heads(mixed, masks).astype(BF16)
        return carry

    lax.fori_loop(0, count, window, 0)
    z = mm(att_ref[...], wo_ref[...]).astype(BF16)
    hidden = state_ref[...] + z.astype(F32)
    centred, inv = norm_stats(hidden)
    unit = centred * inv
    normed2 = (unit * gain2_ref[...]).astype(BF16)
    cot = cot_ref[...]
    mixed_ref[...] = hidden
    state_ref[...] = unit
    d_normed = jnp.zeros((tokens, width), F32)
    chunk = 512
    for c in range(wup_ref.shape[1] // chunk):
        cols = slice(c * chunk, (c + 1) * chunk)
        act, slope = gelu_and_slope(mm(normed2, wup_ref[:, cols]))
        mixed_ref[...] += mm(act.astype(BF16), wdn_ref[cols, :])
        d_up = mm_nt(cot, wdn_ref[cols, :]) * slope
        d_normed += mm_nt(d_up.astype(BF16), wup_ref[:, cols])
    d_unit = d_normed * gain2_ref[...]
    unit = state_ref[...]
    first = jnp.sum(d_unit, axis=1, keepdims=True) * (1.0 / width)
    second = jnp.sum(d_unit * unit, axis=1, keepdims=True) * (1.0 / width)
    d_hidden = cot.astype(F32) + inv * (d_unit - first - unit * second)
    datt_ref[...] = mm_nt(d_hidden.astype(BF16), wo_ref[...]).astype(BF16)


def backward_kernel(
    normed_ref, low_ref, qk_ref, v_ref, probs_ref, datt_ref, up_ref, scale_ref, ids_ref,
    terms_ref,
    qs_ref, kn_ref, dq_ref, dk_ref, dqkv_ref,
):
    tokens, width = normed_ref.shape
    count = tokens // TOKENS
    groups = width // LANES
    masks = head_masks()
    scale = scale_ref[...]
    inv = []
    for part in range(2):
        raw = qk_ref[:, part * width : (part + 1) * width]
        inv.append(lax.rsqrt(head_mean(raw * raw) + 1e-06))
        if part == 0:
            qs_ref[...] = raw * inv[0] * scale
        else:
            kn_ref[...] = (raw * inv[1]).astype(BF16)

    def window(w, carry):
        rows = pl.ds(pl.multiple_of(w * TOKENS, TOKENS), TOKENS)
        for g in range(groups):
            cols = slice(g * LANES, (g + 1) * LANES)
            d_stack = stack_heads(datt_ref[rows, cols].astype(F32), masks)
            q_stack = stack_heads(qs_ref[rows, cols], masks)
            probs = probs_ref[w * groups + g]
            d_probs = mm_nt(v_ref[rows, cols], d_stack)
            wide = probs.astype(F32)
            prod = wide * d_probs
            d_scores = (prod - wide * jnp.sum(prod, axis=0, keepdims=True)).astype(BF16)
            dqkv_ref[rows, slice(2 * width + g * LANES, 2 * width + (g + 1) * LANES)] = mm(
                probs, d_stack
            ).astype(BF16)
            dk_ref[rows, cols] = mm(d_scores, q_stack)
            dq_ref[rows, cols] = unstack_heads(mm_tn(d_scores, kn_ref[rows, cols]), masks)
        return carry

    lax.fori_loop(0, count, window, 0)
    for part, grad_ref in enumerate((dq_ref, dk_ref)):
        cols = slice(part * width, (part + 1) * width)
        unit = qk_ref[:, cols] * inv[part]
        grad = grad_ref[...] * scale if part == 0 else grad_ref[...]
        dqkv_ref[:, cols] = (inv[part] * (grad - unit * head_mean(grad * unit))).astype(BF16)
    low = low_ref[...]
    d_qkv = dqkv_ref[...]
    own = window_columns(tokens, up_ref.shape[0])
    back = (mm_nt(d_qkv, up_ref[...]) * own).astype(BF16)
    grads = jnp.concatenate([mm_tn(back, normed_ref[...]), mm_tn(low, d_qkv)], axis=1)
    blocks = grads.shape[1] // LANES
    for r in range(grads.shape[0] // count):
        for b in range(blocks):
            terms_ref[r * blocks + b, :count, :] = grads[
                r * count : (r + 1) * count, b * LANES : (b + 1) * LANES
            ]
            terms_ref[r * blocks + b, count:, :] = ids_ref[...]


def reduce_kernel(terms_ref, sums_ref):
    pieces, regions = sums_ref.shape[:2]
    half = terms_ref.shape[2] // 2
    for p in range(pieces):
        tile = terms_ref[:, p]
        ids = pltpu.roll(tile, half, 1)
        row = lax.broadcasted_iota(jnp.int32, tile.shape, 1)
        value = jnp.where(row < half, tile, 0.0)
        for g in range(regions):
            part = jnp.sum(jnp.where(ids == g, value, 0.0), axis=0)
            sums_ref[p, g : g + 1, :] = jnp.sum(part, axis=0, keepdims=True).astype(sums_ref.dtype)


def scale_kernel(sums_ref, down_ref, up_ref):
    regions, rank, width = down_ref.shape
    blocks = sums_ref.shape[0] // rank
    total = jnp.zeros((regions, LANES), F32)
    for p in range(sums_ref.shape[0]):
        part = sums_ref[p].astype(F32)
        total += part * part
    size = sums_ref.shape[0] * regions * LANES
    total = jnp.sum(jnp.sum(total, axis=0, keepdims=True), axis=1, keepdims=True)
    factor = lax.rsqrt(total * (1.0 / size) + 1e-06)
    for b in range(blocks):
        part = jnp.stack([sums_ref[r * blocks + b].astype(F32) * factor for r in range(rank)])
        part = jnp.swapaxes(part, 0, 1)
        start = b * LANES
        if start < width:
            down_ref[:, :, start : start + LANES] = part
        else:
            up_ref[:, :, start - width : start - width + LANES] = part


def call(kernel, outs, scratch=(), flops=0, moved=0, name=None):
    return pl.pallas_call(
        kernel,
        out_shape=outs,
        scratch_shapes=list(scratch),
        compiler_params=pltpu.CompilerParams(vmem_limit_bytes=VMEM_LIMIT),
        cost_estimate=pl.CostEstimate(flops=flops, bytes_accessed=moved, transcendentals=0),
        name=name,
    )


def shape(*dims, dtype=F32):
    return jax.ShapeDtypeStruct(dims, dtype)


def halo_pairs(step):
    lats, lons = lax.axis_size("lat"), lax.axis_size("lon")

    def index(a, b):
        return (a % lats) * lons + b % lons

    return [
        (index(a, b), index(a + step[0], b + step[1])) for a in range(lats) for b in range(lons)
    ]


def move(array, step):
    return lax.ppermute(array, ("lat", "lon"), halo_pairs(step))


def to_windows(field):
    levels, rows, cols, width = field.shape
    field = jnp.roll(field, -(WLEV // 2), axis=0)
    field = field.reshape(levels // WLEV, WLEV, rows // WLAT, WLAT, cols // WLON, WLON, width)
    return field.transpose(0, 2, 4, 1, 3, 5, 6).reshape(-1, width)


def from_windows(tokens, levels, rows, cols):
    width = tokens.shape[-1]
    field = tokens.reshape(levels // WLEV, rows // WLAT, cols // WLON, WLEV, WLAT, WLON, width)
    field = field.transpose(0, 3, 1, 4, 2, 5, 6).reshape(levels, rows, cols, width)
    return jnp.roll(field, WLEV // 2, axis=0)


def shifted_windows(field):
    south = move(field[:, :HALF_LAT, HALF_LON:], (-1, 0))
    east = move(field[:, HALF_LAT:, :HALF_LON], (0, -1))
    corner = move(field[:, :HALF_LAT, :HALF_LON], (-1, -1))
    upper = jnp.concatenate((field[:, HALF_LAT:, HALF_LON:], east), axis=2)
    lower = jnp.concatenate((south, corner), axis=2)
    return to_windows(jnp.concatenate((upper, lower), axis=1))


def home_field(tokens, levels, rows, cols):
    field = from_windows(tokens, levels, rows, cols)
    edge = cols - HALF_LON
    north = move(field[:, HALF_LAT:, :edge].astype(BF16), (1, 0)).astype(F32)
    west = move(field[:, :HALF_LAT, edge:].astype(BF16), (0, 1)).astype(F32)
    corner = move(field[:, HALF_LAT:, edge:].astype(BF16), (1, 1)).astype(F32)
    upper = jnp.concatenate((corner, north), axis=2)
    lower = jnp.concatenate((west, field[:, :HALF_LAT, :edge]), axis=2)
    return jnp.concatenate((upper, lower), axis=1)


def same_group(levels, rows):
    level = jnp.arange(levels).reshape(levels // WLEV, WLEV, 1, 1) == levels - 1
    row = jnp.arange(rows).reshape(1, 1, rows, 1) >= rows - HALF_LAT
    row = row & (lax.axis_index("lat") == lax.axis_size("lat") - 1)
    group = jnp.broadcast_to(2 * level + row, (levels // WLEV, WLEV, rows, WLON))
    group = group.reshape(levels // WLEV, TOKENS)
    same = (group[:, :, None] == group[:, None, :]).astype(F32)
    return jnp.tile(same, (1, 1, PER_GROUP))


def local(
    pixels,
    land_patch_mask,
    region,
    patch_embed_weight,
    patch_embed_bias,
    land_embedding_vector,
    attention_norm_gain,
    query_key_value_weight,
    region_down_factor,
    region_up_factor,
    head_logit_scale,
    attention_output_weight,
    feedforward_gain,
    feedforward_up_weight,
    feedforward_down_weight,
    cotangent,
):
    levels, rows, cols, patch_len = pixels.shape
    width = patch_embed_weight.shape[1]
    inner = feedforward_up_weight.shape[1]
    regions, rank, _ = region_down_factor.shape
    region_index = region.reshape(-1)
    count = region_index.shape[0]
    tokens = count * TOKENS
    groups = width // LANES
    devices = lax.axis_size("lat") * lax.axis_size("lon")
    padded = -(-patch_len // LANES) * LANES

    land = jnp.broadcast_to(land_patch_mask.astype(BF16)[None, :, :, None], (levels, rows, cols, 1))
    spare = jnp.zeros((levels, rows, cols, padded - patch_len - 1), BF16)
    pix = shifted_windows(jnp.concatenate((pixels, land, spare), axis=3))
    cot = shifted_windows(cotangent.astype(BF16))
    embed_weight = jnp.pad(patch_embed_weight, ((0, padded - patch_len), (0, 0)))
    down = jnp.take(region_down_factor, region_index, axis=0).swapaxes(0, 1).reshape(-1, width)
    up = jnp.take(region_up_factor, region_index, axis=0).swapaxes(0, 1).reshape(-1, 3 * width)
    scale = jnp.repeat(head_logit_scale / HEAD, HEAD)[None]
    ids = jnp.broadcast_to(region_index.astype(F32)[:, None], (count, LANES))

    mixed, normed, low, qk, v, probs, d_att = call(
        forward_kernel,
        (
            shape(tokens, width),
            shape(tokens, width, dtype=BF16),
            shape(tokens, rank * count, dtype=BF16),
            shape(tokens, 2 * width),
            shape(tokens, width, dtype=BF16),
            shape(count * groups, TOKENS, PER_GROUP * TOKENS, dtype=BF16),
            shape(tokens, width, dtype=BF16),
        ),
        (
            pltpu.VMEM((tokens, width), F32),
            pltpu.VMEM((tokens, width), F32),
            pltpu.VMEM((tokens, width), BF16),
            pltpu.VMEM((tokens, width), BF16),
        ),
        flops=2 * tokens * width * (6 * width + 4 * inner),
        moved=20_000_000,
        name="layer_forward",
    )(
        pix, embed_weight, patch_embed_bias[None], land_embedding_vector[None],
        attention_norm_gain[None], query_key_value_weight, down, up, scale,
        same_group(levels, rows), attention_output_weight, feedforward_gain[None],
        feedforward_up_weight, feedforward_down_weight, cot,
    )
    pieces = rank * 4 * width // LANES
    terms = call(
        backward_kernel,
        shape(pieces, 2 * count, LANES),
        (
            pltpu.VMEM((tokens, width), F32),
            pltpu.VMEM((tokens, width), BF16),
            pltpu.VMEM((tokens, width), F32),
            pltpu.VMEM((tokens, width), F32),
            pltpu.VMEM((tokens, 3 * width), BF16),
        ),
        flops=2 * tokens * width * 4 * width,
        moved=12_000_000,
        name="attention_backward",
    )(normed, low, qk, v, probs, d_att, up, scale, ids)
    mixed_state = home_field(mixed, levels, rows, cols)

    each = pieces // devices
    terms = lax.all_to_all(terms, ("lat", "lon"), 0, 0, tiled=True)
    terms = terms.reshape(devices, each, 2 * count, LANES)
    sums = call(reduce_kernel, shape(each, regions, LANES, dtype=BF16), name="sum_by_region")(terms)
    sums = jnp.broadcast_to(sums[None], (devices, each, regions, LANES))
    sums = lax.all_to_all(sums, ("lat", "lon"), 0, 0, tiled=True)
    step_down, step_up = call(
        scale_kernel,
        (shape(regions, rank, width), shape(regions, rank, 3 * width)),
        name="scale_steps",
    )(sums.reshape(pieces, regions, LANES))
    return (mixed_state, step_down, step_up)


def solution(mesh):
    field = P(None, "lat", "lon", None)
    placed = (field, P("lat", "lon"), P(None, "lat", "lon")) + (P(),) * 12 + (field,)
    return jax.shard_map(
        local, mesh=mesh, in_specs=placed, out_specs=(field, P(), P()), check_vma=False
    )
```

```python
import jax
import jax.numpy as jnp
from jax import lax
from jax.experimental import pallas as pl
from jax.experimental.pallas import tpu as pltpu
from jax.sharding import PartitionSpec as P

WLEV = 2
WLAT = 6
WLON = 12
TOKENS = WLEV * WLAT * WLON
HALF_LAT = WLAT // 2
HALF_LON = WLON // 2
LANES = 128
HEAD = 32
PER_GROUP = LANES // HEAD

AXES = ("lat", "lon")
F32 = jnp.float32
BF16 = jnp.bfloat16


def mm(a, b):
    return lax.dot_general(a, b, (((1,), (0,)), ((), ())), preferred_element_type=F32)


def mm_nt(a, b):
    return lax.dot_general(a, b, (((1,), (1,)), ((), ())), preferred_element_type=F32)


def mm_tn(a, b):
    return lax.dot_general(a, b, (((0,), (0,)), ((), ())), preferred_element_type=F32)


def head_mean(squares):
    rows = lax.broadcasted_iota(jnp.int32, (LANES, LANES), 0) // HEAD
    cols = lax.broadcasted_iota(jnp.int32, (LANES, LANES), 1) // HEAD
    block = jnp.where(rows == cols, 1.0 / HEAD, 0.0).astype(BF16)
    parts = []
    for g in range(squares.shape[1] // LANES):
        part = squares[:, g * LANES : (g + 1) * LANES]
        top = part.astype(BF16)
        rest = (part - top.astype(F32)).astype(BF16)
        parts.append(mm(top, block) + mm(rest, block))
    return jnp.concatenate(parts, axis=1)


def head_masks():
    lane = lax.broadcasted_iota(jnp.int32, (1, LANES), 1) // HEAD
    return [jnp.where(lane == h, 1.0, 0.0).astype(F32) for h in range(PER_GROUP)]


def stack_heads(x, masks):
    return jnp.concatenate([(x * m).astype(BF16) for m in masks], axis=0)


def unstack_heads(x, masks):
    tokens = x.shape[0] // PER_GROUP
    return sum(x[h * tokens : (h + 1) * tokens] * m for h, m in enumerate(masks))


def adapter_columns(tokens, columns):
    rank = columns // (tokens // TOKENS)
    own = lax.broadcasted_iota(jnp.int32, (tokens, columns), 0)
    first = lax.broadcasted_iota(jnp.int32, (tokens, columns), 1) // rank * TOKENS
    return jnp.where((own >= first) & (own < first + TOKENS), 1.0, 0.0)


def factors(region_ref, factor_ref, all_ref):
    rank = factor_ref.shape[1]
    ids = [region_ref[a, 0, b] for a in range(region_ref.shape[0]) for b in range(region_ref.shape[2])]
    for w, r in enumerate(ids):
        all_ref[w * rank : (w + 1) * rank, :] = factor_ref[r].astype(F32)
    return all_ref[...].astype(BF16)


def scale_row(scale_ref, width):
    head = lax.broadcasted_iota(jnp.int32, (1, width), 1) // HEAD
    row = jnp.zeros((1, width), F32)
    for h in range(width // HEAD):
        row = jnp.where(head == h, scale_ref[h] / HEAD, row)
    return row


def same_group(level, south):
    def group(token):
        late = jnp.where(token >= TOKENS // WLEV, 1, 0) * level
        low = jnp.where(token // WLON % WLAT >= HALF_LAT, 1, 0) * south
        return 2 * late + low

    keys = lax.broadcasted_iota(jnp.int32, (TOKENS, 1), 0)
    queries = lax.broadcasted_iota(jnp.int32, (1, PER_GROUP * TOKENS), 1) % TOKENS
    return jnp.where(group(keys) == group(queries), 1.0, 0.0)


def pieces_of(shape):
    levels, _, cols, _ = shape
    across = (cols + HALF_LON) // WLON
    for level in range(levels):
        for row in range(WLAT):
            within = level % WLEV * WLAT * WLON + row * WLON
            starts = [((level // WLEV) * across + b) * TOKENS + within for b in range(across)]
            yield (level + WLEV // 2) % levels, row // HALF_LAT, row % HALF_LAT, starts


def into_windows(stage_ref, own_ref, south_ref, east_ref, corner_ref):
    for level, half, row, starts in pieces_of(own_ref.shape):
        wide = (south_ref if half else own_ref)[level, row].astype(F32)
        narrow = (corner_ref if half else east_ref)[level, row].astype(F32)
        for b, start in enumerate(starts[:-1]):
            stage_ref[start : start + WLON, :] = wide[b * WLON : (b + 1) * WLON]
        start = starts[-1]
        stage_ref[start : start + HALF_LON, :] = wide[-HALF_LON:]
        stage_ref[start + HALF_LON : start + WLON, :] = narrow


def out_of_windows(stage_ref, own_ref, north_ref, west_ref, corner_ref):
    for level, half, row, starts in pieces_of(own_ref.shape):
        wide = [stage_ref[start : start + WLON, :] for start in starts[:-1]]
        start = starts[-1]
        wide.append(stage_ref[start : start + HALF_LON, :])
        narrow = stage_ref[start + HALF_LON : start + WLON, :]
        wide_ref, narrow_ref = (north_ref, corner_ref) if half else (own_ref, west_ref)
        wide_ref[level, row] = jnp.concatenate(wide, axis=0).astype(wide_ref.dtype)
        narrow_ref[level, row] = narrow.astype(narrow_ref.dtype)


def norm_stats(x):
    width = x.shape[1]
    mean = jnp.sum(x, axis=1, keepdims=True) * (1.0 / width)
    centred = x - mean
    spread = jnp.sum(centred * centred, axis=1, keepdims=True) * (1.0 / width)
    return centred, lax.rsqrt(spread + 1e-05)


def gelu_and_slope(u):
    x = jnp.abs(u) * 0.7071067811865476
    t = 1.0 / (1.0 + 0.3275911 * x)
    e = jnp.exp(-0.5 * u * u)
    poly = 1.061405429
    for c in (-1.453152027, 1.421413741, -0.284496736, 0.254829592):
        poly = poly * t + c
    tail = 0.5 * poly * t * e
    phi = jnp.where(u < 0, tail, 1.0 - tail)
    return u * phi, phi + u * (0.3989422804014327 * e)


def attention_kernel(
    region_ref, temper_ref, own_ref, south_ref, east_ref, corner_ref, wp_ref, bias_ref, land_ref,
    gain_ref, wqkv_ref, down_ref, up_ref, wo_ref,
    hidden_ref, normed_ref, low_ref, qk_ref, v_ref, probs_ref,
    state_ref, qs_ref, kn_ref, att_ref, downs_ref, ups_ref, same_ref,
):
    tokens, width = state_ref.shape
    count = tokens // TOKENS
    groups = width // LANES
    masks = head_masks()
    patch_len = wp_ref.shape[0]
    into_windows(state_ref, own_ref, south_ref, east_ref, corner_ref)
    pix = state_ref[:, :patch_len].astype(BF16)
    land = state_ref[:, patch_len : patch_len + 1]
    state = mm(pix, wp_ref[...]) + bias_ref[...] + land * land_ref[...]
    state_ref[...] = state
    centred, inv = norm_stats(state)
    normed = (centred * inv * gain_ref[...]).astype(BF16)
    normed_ref[...] = normed
    downs = factors(region_ref, down_ref, downs_ref)
    ups = factors(region_ref, up_ref, ups_ref)
    low = (mm_nt(normed, downs) * adapter_columns(tokens, downs.shape[0])).astype(BF16)
    low_ref[...] = low
    scale = scale_row(temper_ref, width)
    for part in range(3):
        cols = slice(part * width, (part + 1) * width)
        qkv = mm(normed, wqkv_ref[:, cols]) + mm(low, ups[:, cols])
        if part == 2:
            v_ref[...] = qkv.astype(BF16)
        else:
            qk_ref[:, cols] = qkv
            unit = qkv * lax.rsqrt(head_mean(qkv * qkv) + 1e-06)
            if part == 0:
                qs_ref[...] = unit * scale
            else:
                kn_ref[...] = unit.astype(BF16)
    last_band = lax.axis_index("lat") == lax.axis_size("lat") - 1
    south = jnp.where(last_band, 1, 0).astype(jnp.int32)
    parts = same_ref.shape[0]
    for part in range(parts):
        same_ref[part] = same_group(1 if part == parts - 1 else 0, south)

    def window(w, carry):
        rows = pl.ds(pl.multiple_of(w * TOKENS, TOKENS), TOKENS)
        same = same_ref[w // (count // parts)]
        for g in range(groups):
            cols = slice(g * LANES, (g + 1) * LANES)
            stack = stack_heads(qs_ref[rows, cols], masks)
            weights = jnp.exp(mm_nt(kn_ref[rows, cols], stack)) * same
            total = jnp.sum(weights, axis=0, keepdims=True)
            probs = (weights * (1.0 / total)).astype(BF16)
            probs_ref[w * groups + g] = probs
            mixed = mm_tn(probs, v_ref[rows, cols])
            att_ref[rows, cols] = unstack_heads(mixed, masks).astype(BF16)
        return carry

    lax.fori_loop(0, count, window, 0)
    z = mm(att_ref[...], wo_ref[...]).astype(BF16)
    hidden_ref[...] = state_ref[...] + z.astype(F32)


def feed_kernel(
    hidden_ref, own_ref, south_ref, east_ref, corner_ref, gain_ref, wup_ref, wdn_ref, wo_ref,
    home_ref, north_ref, west_ref, diagonal_ref, datt_ref,
    cot_ref, mixed_ref, unit_ref,
):
    tokens, width = hidden_ref.shape
    into_windows(cot_ref, own_ref, south_ref, east_ref, corner_ref)
    hidden = hidden_ref[...]
    centred, inv = norm_stats(hidden)
    unit = centred * inv
    normed = (unit * gain_ref[...]).astype(BF16)
    cot = cot_ref[...].astype(BF16)
    mixed_ref[...] = hidden
    unit_ref[...] = unit
    d_normed = jnp.zeros((tokens, width), F32)
    chunk = 512
    for c in range(wup_ref.shape[1] // chunk):
        cols = slice(c * chunk, (c + 1) * chunk)
        act, slope = gelu_and_slope(mm(normed, wup_ref[:, cols]))
        mixed_ref[...] += mm(act.astype(BF16), wdn_ref[cols, :])
        d_up = mm_nt(cot, wdn_ref[cols, :]) * slope
        d_normed += mm_nt(d_up.astype(BF16), wup_ref[:, cols])
    out_of_windows(mixed_ref, home_ref, north_ref, west_ref, diagonal_ref)
    d_unit = d_normed * gain_ref[...]
    unit = unit_ref[...]
    first = jnp.sum(d_unit, axis=1, keepdims=True) * (1.0 / width)
    second = jnp.sum(d_unit * unit, axis=1, keepdims=True) * (1.0 / width)
    d_hidden = cot_ref[...] + inv * (d_unit - first - unit * second)
    datt_ref[...] = mm_nt(d_hidden.astype(BF16), wo_ref[...]).astype(BF16)


def backward_kernel(
    region_ref, temper_ref, normed_ref, low_ref, qk_ref, v_ref, probs_ref, datt_ref, up_ref,
    terms_ref,
    qs_ref, kn_ref, dq_ref, dk_ref, dqkv_ref, ups_ref, grads_ref,
):
    tokens, width = normed_ref.shape
    count = tokens // TOKENS
    groups = width // LANES
    masks = head_masks()
    scale = scale_row(temper_ref, width)
    inv = []
    for part in range(2):
        raw = qk_ref[:, part * width : (part + 1) * width]
        inv.append(lax.rsqrt(head_mean(raw * raw) + 1e-06))
        if part == 0:
            qs_ref[...] = raw * inv[0] * scale
        else:
            kn_ref[...] = (raw * inv[1]).astype(BF16)

    def window(w, carry):
        rows = pl.ds(pl.multiple_of(w * TOKENS, TOKENS), TOKENS)
        for g in range(groups):
            cols = slice(g * LANES, (g + 1) * LANES)
            d_stack = stack_heads(datt_ref[rows, cols].astype(F32), masks)
            q_stack = stack_heads(qs_ref[rows, cols], masks)
            probs = probs_ref[w * groups + g]
            d_probs = mm_nt(v_ref[rows, cols], d_stack)
            wide = probs.astype(F32)
            prod = wide * d_probs
            d_scores = (prod - wide * jnp.sum(prod, axis=0, keepdims=True)).astype(BF16)
            dqkv_ref[rows, slice(2 * width + g * LANES, 2 * width + (g + 1) * LANES)] = mm(
                probs, d_stack
            ).astype(BF16)
            dk_ref[rows, cols] = mm(d_scores, q_stack)
            dq_ref[rows, cols] = unstack_heads(mm_tn(d_scores, kn_ref[rows, cols]), masks)
        return carry

    lax.fori_loop(0, count, window, 0)
    for part, grad_ref in enumerate((dq_ref, dk_ref)):
        cols = slice(part * width, (part + 1) * width)
        unit = qk_ref[:, cols] * inv[part]
        grad = grad_ref[...] * scale if part == 0 else grad_ref[...]
        dqkv_ref[:, cols] = (inv[part] * (grad - unit * head_mean(grad * unit))).astype(BF16)
    ups = factors(region_ref, up_ref, ups_ref)
    d_qkv = dqkv_ref[...]
    back = (mm_nt(d_qkv, ups) * adapter_columns(tokens, ups.shape[0])).astype(BF16)
    grads_ref[:, :width] = mm_tn(back, normed_ref[...])
    grads_ref[:, width:] = mm_tn(low_ref[...], d_qkv)
    blocks = grads_ref.shape[1] // LANES
    rank = grads_ref.shape[0] // count
    row = lax.broadcasted_iota(jnp.int32, (count, LANES), 0)
    ids = jnp.zeros((count, LANES), F32)
    per = region_ref.shape[2]
    for w in range(count):
        ids = jnp.where(row == w, region_ref[w // per, 0, w % per].astype(F32), ids)
    for b in range(blocks):
        cols = slice(b * LANES, (b + 1) * LANES)
        for r in range(rank):
            own = [grads_ref[w * rank + r : w * rank + r + 1, cols] for w in range(count)]
            tile = jnp.concatenate(own + [ids], axis=0)
            terms_ref[r * blocks + b] = tile.astype(terms_ref.dtype)


def reduce_kernel(terms_ref, sums_ref):
    _, pieces, regions, _ = sums_ref.shape
    devices, _, height, _ = terms_ref.shape
    for p in range(pieces):
        tile = terms_ref[:, p].astype(F32).reshape(devices * height, LANES)
        ids = pltpu.roll(tile, devices * height - height // 2, 0)
        row = lax.broadcasted_iota(jnp.int32, tile.shape, 0) % height
        lane = lax.broadcasted_iota(jnp.int32, tile.shape, 1).astype(F32)
        hot = jnp.where((ids == lane) & (row < height // 2), 1.0, 0.0).astype(BF16)
        sums = mm_tn(hot, tile.astype(BF16))[:regions].astype(sums_ref.dtype)
        for d in range(sums_ref.shape[0]):
            sums_ref[d, p] = sums


def scale_kernel(near_ref, far_ref, down_ref, up_ref, all_ref):
    regions, _, width = down_ref.shape
    rank, blocks = all_ref.shape[:2]
    outer, inner = near_ref.shape[:2]
    core = lax.axis_index("lat") % 2
    total = jnp.zeros((regions, LANES), F32)
    for side, ref in enumerate((near_ref, far_ref)):
        which = core if side == 0 else 1 - core
        for a in range(outer):
            for r in range(inner):
                for b in range(blocks):
                    part = ref[a, r, b].astype(F32)
                    total += part * part
                    all_ref[(a * 2 + which) * inner + r, b] = part
    size = rank * blocks * regions * LANES
    total = jnp.sum(jnp.sum(total, axis=0, keepdims=True), axis=1, keepdims=True)
    factor = lax.rsqrt(total * (1.0 / size) + 1e-06)
    for b in range(blocks):
        part = jnp.swapaxes(all_ref[:, b] * factor, 0, 1)
        start = b * LANES
        if start < width:
            down_ref[:, :, start : start + LANES] = part
        else:
            up_ref[:, :, start - width : start - width + LANES] = part


SMEM = pl.BlockSpec(memory_space=pltpu.SMEM)
VMEM = pl.BlockSpec(memory_space=pltpu.VMEM)


def call(kernel, places, outs, scratch=(), flops=0, moved=0, mib=32, name=None):
    return pl.pallas_call(
        kernel,
        in_specs=places,
        out_shape=outs,
        scratch_shapes=[pltpu.VMEM(dims, dtype) for dims, dtype in scratch],
        compiler_params=pltpu.CompilerParams(vmem_limit_bytes=mib * 1024 * 1024),
        cost_estimate=pl.CostEstimate(flops=flops, bytes_accessed=moved, transcendentals=0),
        name=name,
    )


def shape(*dims, dtype=F32):
    return jax.ShapeDtypeStruct(dims, dtype)


def move(array, step):
    lats, lons = lax.axis_size("lat"), lax.axis_size("lon")

    def index(a, b):
        return (a % lats) * lons + b % lons

    pairs = [
        (index(a, b), index(a + step[0], b + step[1])) for a in range(lats) for b in range(lons)
    ]
    return lax.ppermute(array, ("lat", "lon"), pairs)


def halves(field):
    south = move(field[:, :HALF_LAT, HALF_LON:], (-1, 0))
    east = move(field[:, HALF_LAT:, :HALF_LON], (0, -1))
    corner = move(field[:, :HALF_LAT, :HALF_LON], (-1, -1))
    return field[:, HALF_LAT:, HALF_LON:], south, east, corner


def local(
    pixels,
    land_patch_mask,
    region,
    patch_embed_weight,
    patch_embed_bias,
    land_embedding_vector,
    attention_norm_gain,
    query_key_value_weight,
    region_down_factor,
    region_up_factor,
    head_logit_scale,
    attention_output_weight,
    feedforward_gain,
    feedforward_up_weight,
    feedforward_down_weight,
    cotangent,
):
    levels, rows, cols, patch_len = pixels.shape
    width = patch_embed_weight.shape[1]
    inner = feedforward_up_weight.shape[1]
    regions, rank, _ = region_down_factor.shape
    count = region.size
    tokens = count * TOKENS
    groups = width // LANES
    devices = lax.axis_size("lat") * lax.axis_size("lon")
    spare = width - patch_len - 1

    land = jnp.broadcast_to(land_patch_mask.astype(BF16)[None, :, :, None], (levels, rows, cols, 1))
    blank = jnp.zeros((levels, rows, cols, spare), BF16)
    pix = halves(jnp.concatenate((pixels, land, blank), axis=3))
    cot = halves(cotangent.astype(BF16))

    wide = (levels, HALF_LAT, cols - HALF_LON, width)
    narrow = (levels, HALF_LAT, HALF_LON, width)
    hidden, normed, low, qk, v, probs = call(
        attention_kernel,
        [SMEM] * 2 + [VMEM] * 12,
        (
            shape(tokens, width),
            shape(tokens, width, dtype=BF16),
            shape(tokens, rank * count, dtype=BF16),
            shape(tokens, 2 * width),
            shape(tokens, width, dtype=BF16),
            shape(count * groups, TOKENS, PER_GROUP * TOKENS, dtype=BF16),
        ),
        (
            ((tokens, width), F32),
            ((tokens, width), F32),
            ((tokens, width), BF16),
            ((tokens, width), BF16),
            ((rank * count, width), F32),
            ((rank * count, 3 * width), F32),
            ((levels // WLEV, TOKENS, PER_GROUP * TOKENS), F32),
        ),
        flops=2 * tokens * width * 6 * width,
        moved=20_000_000,
        name="attention_forward",
    )(
        region, head_logit_scale, *pix, patch_embed_weight, patch_embed_bias[None],
        land_embedding_vector[None], attention_norm_gain[None], query_key_value_weight,
        region_down_factor, region_up_factor, attention_output_weight,
    )
    home, north, west, diagonal, d_att = call(
        feed_kernel,
        [VMEM] * 9,
        (
            shape(*wide),
            shape(*wide, dtype=BF16),
            shape(*narrow, dtype=BF16),
            shape(*narrow, dtype=BF16),
            shape(tokens, width, dtype=BF16),
        ),
        (((tokens, width), F32),) * 3,
        flops=2 * tokens * width * 4 * inner,
        moved=20_000_000,
        name="feed_forward",
    )(
        hidden, *cot, feedforward_gain[None], feedforward_up_weight, feedforward_down_weight,
        attention_output_weight,
    )
    north = move(north, (1, 0)).astype(F32)
    west = move(west, (0, 1)).astype(F32)
    diagonal = move(diagonal, (1, 1)).astype(F32)
    pieces = rank * 4 * width // LANES
    terms = call(
        backward_kernel,
        [SMEM] * 2 + [VMEM] * 7,
        shape(pieces, 2 * count, LANES, dtype=BF16),
        (
            ((tokens, width), F32),
            ((tokens, width), BF16),
            ((tokens, width), F32),
            ((tokens, width), F32),
            ((tokens, 3 * width), BF16),
            ((rank * count, 3 * width), F32),
            ((rank * count, 4 * width), F32),
        ),
        flops=2 * tokens * width * 4 * width,
        moved=12_000_000,
        name="attention_backward",
    )(region, head_logit_scale, normed, low, qk, v, probs, d_att, region_up_factor)
    upper = jnp.concatenate((diagonal, north), axis=2)
    lower = jnp.concatenate((west, home), axis=2)
    mixed_state = jnp.concatenate((upper, lower), axis=1)

    each = pieces // devices
    terms = lax.all_to_all(terms, AXES, 0, 0, tiled=True)
    sums = call(
        reduce_kernel,
        [VMEM],
        shape(devices // 2, each, regions, LANES, dtype=BF16),
        name="sum_by_region",
    )(terms.reshape(devices, each, 2 * count, LANES))
    lats, lons = lax.axis_size("lat"), lax.axis_size("lon")
    cores = [[a * lons + b for a in range(c, lats, 2) for b in range(lons)] for c in range(2)]
    near = lax.all_to_all(sums, AXES, 0, 0, axis_index_groups=cores, tiled=True)
    far = lax.ppermute(near, "lat", [(a, a ^ 1) for a in range(lats)])
    blocks = 4 * width // LANES
    order = (lats // 2, rank // lats, blocks, regions, LANES)
    step_down, step_up = call(
        scale_kernel,
        [VMEM] * 2,
        (shape(regions, rank, width), shape(regions, rank, 3 * width)),
        (((rank, blocks, regions, LANES), F32),),
        name="scale_steps",
    )(near.reshape(order), far.reshape(order))
    return (mixed_state, step_down, step_up)


def solution(mesh):
    field = P(None, "lat", "lon", None)
    placed = (field, P("lat", "lon"), P(None, "lat", "lon")) + (P(),) * 12 + (field,)
    return jax.shard_map(
        local, mesh=mesh, in_specs=placed, out_specs=(field, P(), P()), check_vma=False
    )
```

```python
import jax
import jax.numpy as jnp
from jax import lax
from jax.experimental import pallas as pl
from jax.experimental.pallas import tpu as pltpu
from jax.sharding import PartitionSpec as P

WLEV = 2
WLAT = 6
WLON = 12
TOKENS = WLEV * WLAT * WLON
HALF_LAT = WLAT // 2
HALF_LON = WLON // 2
LANES = 128
HEAD = 32
PER_GROUP = LANES // HEAD

AXES = ("lat", "lon")
F32 = jnp.float32
BF16 = jnp.bfloat16


def mm(a, b):
    return lax.dot_general(a, b, (((1,), (0,)), ((), ())), preferred_element_type=F32)


def mm_nt(a, b):
    return lax.dot_general(a, b, (((1,), (1,)), ((), ())), preferred_element_type=F32)


def mm_tn(a, b):
    return lax.dot_general(a, b, (((0,), (0,)), ((), ())), preferred_element_type=F32)


def head_mean(squares):
    rows = lax.broadcasted_iota(jnp.int32, (LANES, LANES), 0) // HEAD
    cols = lax.broadcasted_iota(jnp.int32, (LANES, LANES), 1) // HEAD
    block = jnp.where(rows == cols, 1.0 / HEAD, 0.0).astype(BF16)
    parts = []
    for g in range(squares.shape[1] // LANES):
        part = squares[:, g * LANES : (g + 1) * LANES]
        top = part.astype(BF16)
        rest = (part - top.astype(F32)).astype(BF16)
        parts.append(mm(top, block) + mm(rest, block))
    return jnp.concatenate(parts, axis=1)


def head_masks():
    lane = lax.broadcasted_iota(jnp.int32, (1, LANES), 1) // HEAD
    return [jnp.where(lane == h, 1.0, 0.0).astype(F32) for h in range(PER_GROUP)]


def stack_heads(x, masks):
    return jnp.concatenate([(x * m).astype(BF16) for m in masks], axis=0)


def unstack_heads(x, masks):
    tokens = x.shape[0] // PER_GROUP
    return sum(x[h * tokens : (h + 1) * tokens] * m for h, m in enumerate(masks))


def adapter_columns(tokens, columns):
    rank = columns // (tokens // TOKENS)
    own = lax.broadcasted_iota(jnp.int32, (tokens, columns), 0)
    first = lax.broadcasted_iota(jnp.int32, (tokens, columns), 1) // rank * TOKENS
    return jnp.where((own >= first) & (own < first + TOKENS), 1.0, 0.0)


def factors(region_ref, factor_ref, all_ref):
    rank = factor_ref.shape[1]
    ids = [region_ref[a, 0, b] for a in range(region_ref.shape[0]) for b in range(region_ref.shape[2])]
    for w, r in enumerate(ids):
        all_ref[w * rank : (w + 1) * rank, :] = factor_ref[r].astype(F32)
    return all_ref[...].astype(BF16)


def scale_row(scale_ref, width):
    head = lax.broadcasted_iota(jnp.int32, (1, width), 1) // HEAD
    row = jnp.zeros((1, width), F32)
    for h in range(width // HEAD):
        row = jnp.where(head == h, scale_ref[h] / HEAD, row)
    return row


def same_group(level, south):
    def group(token):
        late = jnp.where(token >= TOKENS // WLEV, 1, 0) * level
        low = jnp.where(token // WLON % WLAT >= HALF_LAT, 1, 0) * south
        return 2 * late + low

    keys = lax.broadcasted_iota(jnp.int32, (TOKENS, 1), 0)
    queries = lax.broadcasted_iota(jnp.int32, (1, PER_GROUP * TOKENS), 1) % TOKENS
    return jnp.where(group(keys) == group(queries), 1.0, 0.0)


def pieces_of(shape):
    levels, _, cols, _ = shape
    across = (cols + HALF_LON) // WLON
    for level in range(levels):
        for row in range(WLAT):
            within = level % WLEV * WLAT * WLON + row * WLON
            starts = [((level // WLEV) * across + b) * TOKENS + within for b in range(across)]
            yield (level + WLEV // 2) % levels, row // HALF_LAT, row % HALF_LAT, starts


def into_windows(stage_ref, own_ref, south_ref, east_ref, corner_ref):
    for level, half, row, starts in pieces_of(own_ref.shape):
        wide = (south_ref if half else own_ref)[level, row].astype(F32)
        narrow = (corner_ref if half else east_ref)[level, row].astype(F32)
        for b, start in enumerate(starts[:-1]):
            stage_ref[start : start + WLON, :] = wide[b * WLON : (b + 1) * WLON]
        start = starts[-1]
        stage_ref[start : start + HALF_LON, :] = wide[-HALF_LON:]
        stage_ref[start + HALF_LON : start + WLON, :] = narrow


def out_of_windows(stage_ref, own_ref, north_ref, west_ref, corner_ref):
    for level, half, row, starts in pieces_of(own_ref.shape):
        wide = [stage_ref[start : start + WLON, :] for start in starts[:-1]]
        start = starts[-1]
        wide.append(stage_ref[start : start + HALF_LON, :])
        narrow = stage_ref[start + HALF_LON : start + WLON, :]
        wide_ref, narrow_ref = (north_ref, corner_ref) if half else (own_ref, west_ref)
        wide_ref[level, row] = jnp.concatenate(wide, axis=0).astype(wide_ref.dtype)
        narrow_ref[level, row] = narrow.astype(narrow_ref.dtype)


def norm_stats(x):
    width = x.shape[1]
    mean = jnp.sum(x, axis=1, keepdims=True) * (1.0 / width)
    centred = x - mean
    spread = jnp.sum(centred * centred, axis=1, keepdims=True) * (1.0 / width)
    return centred, lax.rsqrt(spread + 1e-05)


def gelu_and_slope(u):
    x = jnp.abs(u) * 0.7071067811865476
    t = 1.0 / (1.0 + 0.3275911 * x)
    e = jnp.exp(-0.5 * u * u)
    poly = 1.061405429
    for c in (-1.453152027, 1.421413741, -0.284496736, 0.254829592):
        poly = poly * t + c
    tail = 0.5 * poly * t * e
    phi = jnp.where(u < 0, tail, 1.0 - tail)
    return u * phi, phi + u * (0.3989422804014327 * e)


def pack_kernel(pixels_ref, land_ref, own_ref, south_ref, east_ref, corner_ref):
    levels, rows, cols, patch_len = pixels_ref.shape
    width = own_ref.shape[3]
    eye = lax.broadcasted_iota(jnp.int32, (cols, cols), 0)
    eye = jnp.where(eye == lax.broadcasted_iota(jnp.int32, (cols, cols), 1), 1.0, 0.0)
    land = mm_nt(eye.astype(BF16), land_ref[...].astype(F32).astype(BF16))
    lane = lax.broadcasted_iota(jnp.int32, (cols, width), 1)
    blank = jnp.zeros((cols, width - patch_len), F32)
    for level in range(levels):
        for row in range(rows):
            patch = jnp.concatenate((pixels_ref[level, row].astype(F32), blank), axis=1)
            patch = jnp.where(lane == patch_len, land[:, row : row + 1], patch).astype(BF16)
            half, at = divmod(row, HALF_LAT)
            (own_ref if half else south_ref)[level, at] = patch[HALF_LON:]
            (east_ref if half else corner_ref)[level, at] = patch[:HALF_LON]


def attention_kernel(
    region_ref, temper_ref, own_ref, south_ref, east_ref, corner_ref, wp_ref, bias_ref, land_ref,
    gain_ref, wqkv_ref, down_ref, up_ref, wo_ref,
    hidden_ref, normed_ref, low_ref, qk_ref, v_ref, probs_ref,
    state_ref, qs_ref, kn_ref, att_ref, downs_ref, ups_ref, same_ref,
):
    tokens, width = state_ref.shape
    count = tokens // TOKENS
    groups = width // LANES
    masks = head_masks()
    patch_len = wp_ref.shape[0]
    into_windows(state_ref, own_ref, south_ref, east_ref, corner_ref)
    pix = state_ref[:, :patch_len].astype(BF16)
    land = state_ref[:, patch_len : patch_len + 1]
    state = mm(pix, wp_ref[...]) + bias_ref[...] + land * land_ref[...]
    state_ref[...] = state
    centred, inv = norm_stats(state)
    normed = (centred * inv * gain_ref[...]).astype(BF16)
    normed_ref[...] = normed
    downs = factors(region_ref, down_ref, downs_ref)
    ups = factors(region_ref, up_ref, ups_ref)
    low = (mm_nt(normed, downs) * adapter_columns(tokens, downs.shape[0])).astype(BF16)
    low_ref[...] = low
    scale = scale_row(temper_ref, width)
    for part in range(3):
        cols = slice(part * width, (part + 1) * width)
        qkv = mm(normed, wqkv_ref[:, cols]) + mm(low, ups[:, cols])
        if part == 2:
            v_ref[...] = qkv.astype(BF16)
        else:
            qk_ref[:, cols] = qkv
            unit = qkv * lax.rsqrt(head_mean(qkv * qkv) + 1e-06)
            if part == 0:
                qs_ref[...] = unit * scale
            else:
                kn_ref[...] = unit.astype(BF16)
    last_band = lax.axis_index("lat") == lax.axis_size("lat") - 1
    south = jnp.where(last_band, 1, 0).astype(jnp.int32)
    parts = same_ref.shape[0]
    for part in range(parts):
        same_ref[part] = same_group(1 if part == parts - 1 else 0, south)

    def window(w, carry):
        rows = pl.ds(pl.multiple_of(w * TOKENS, TOKENS), TOKENS)
        same = same_ref[w // (count // parts)]
        for g in range(groups):
            cols = slice(g * LANES, (g + 1) * LANES)
            stack = stack_heads(qs_ref[rows, cols], masks)
            weights = jnp.exp(mm_nt(kn_ref[rows, cols], stack)) * same
            total = jnp.sum(weights, axis=0, keepdims=True)
            probs = (weights * (1.0 / total)).astype(BF16)
            probs_ref[w * groups + g] = probs
            mixed = mm_tn(probs, v_ref[rows, cols])
            att_ref[rows, cols] = unstack_heads(mixed, masks).astype(BF16)
        return carry

    lax.fori_loop(0, count, window, 0)
    z = mm(att_ref[...], wo_ref[...]).astype(BF16)
    hidden_ref[...] = state_ref[...] + z.astype(F32)


def feed_kernel(
    hidden_ref, own_ref, south_ref, east_ref, corner_ref, gain_ref, wup_ref, wdn_ref, wo_ref,
    home_ref, north_ref, west_ref, diagonal_ref, datt_ref,
    cot_ref, mixed_ref, unit_ref,
):
    tokens, width = hidden_ref.shape
    into_windows(cot_ref, own_ref, south_ref, east_ref, corner_ref)
    hidden = hidden_ref[...]
    centred, inv = norm_stats(hidden)
    unit = centred * inv
    normed = (unit * gain_ref[...]).astype(BF16)
    cot = cot_ref[...].astype(BF16)
    mixed_ref[...] = hidden
    unit_ref[...] = unit
    d_normed = jnp.zeros((tokens, width), F32)
    chunk = 512
    for c in range(wup_ref.shape[1] // chunk):
        cols = slice(c * chunk, (c + 1) * chunk)
        act, slope = gelu_and_slope(mm(normed, wup_ref[:, cols]))
        mixed_ref[...] += mm(act.astype(BF16), wdn_ref[cols, :])
        d_up = mm_nt(cot, wdn_ref[cols, :]) * slope
        d_normed += mm_nt(d_up.astype(BF16), wup_ref[:, cols])
    out_of_windows(mixed_ref, home_ref, north_ref, west_ref, diagonal_ref)
    d_unit = d_normed * gain_ref[...]
    unit = unit_ref[...]
    first = jnp.sum(d_unit, axis=1, keepdims=True) * (1.0 / width)
    second = jnp.sum(d_unit * unit, axis=1, keepdims=True) * (1.0 / width)
    d_hidden = cot_ref[...] + inv * (d_unit - first - unit * second)
    datt_ref[...] = mm_nt(d_hidden.astype(BF16), wo_ref[...]).astype(BF16)


def backward_kernel(
    region_ref, temper_ref, normed_ref, low_ref, qk_ref, v_ref, probs_ref, datt_ref, up_ref,
    terms_ref,
    qs_ref, kn_ref, dq_ref, dk_ref, dqkv_ref, ups_ref, grads_ref,
):
    tokens, width = normed_ref.shape
    count = tokens // TOKENS
    groups = width // LANES
    masks = head_masks()
    scale = scale_row(temper_ref, width)
    inv = []
    for part in range(2):
        raw = qk_ref[:, part * width : (part + 1) * width]
        inv.append(lax.rsqrt(head_mean(raw * raw) + 1e-06))
        if part == 0:
            qs_ref[...] = raw * inv[0] * scale
        else:
            kn_ref[...] = (raw * inv[1]).astype(BF16)

    def window(w, carry):
        rows = pl.ds(pl.multiple_of(w * TOKENS, TOKENS), TOKENS)
        for g in range(groups):
            cols = slice(g * LANES, (g + 1) * LANES)
            d_stack = stack_heads(datt_ref[rows, cols].astype(F32), masks)
            q_stack = stack_heads(qs_ref[rows, cols], masks)
            probs = probs_ref[w * groups + g]
            d_probs = mm_nt(v_ref[rows, cols], d_stack)
            wide = probs.astype(F32)
            prod = wide * d_probs
            d_scores = (prod - wide * jnp.sum(prod, axis=0, keepdims=True)).astype(BF16)
            dqkv_ref[rows, slice(2 * width + g * LANES, 2 * width + (g + 1) * LANES)] = mm(
                probs, d_stack
            ).astype(BF16)
            dk_ref[rows, cols] = mm(d_scores, q_stack)
            dq_ref[rows, cols] = unstack_heads(mm_tn(d_scores, kn_ref[rows, cols]), masks)
        return carry

    lax.fori_loop(0, count, window, 0)
    for part, grad_ref in enumerate((dq_ref, dk_ref)):
        cols = slice(part * width, (part + 1) * width)
        unit = qk_ref[:, cols] * inv[part]
        grad = grad_ref[...] * scale if part == 0 else grad_ref[...]
        dqkv_ref[:, cols] = (inv[part] * (grad - unit * head_mean(grad * unit))).astype(BF16)
    ups = factors(region_ref, up_ref, ups_ref)
    d_qkv = dqkv_ref[...]
    back = (mm_nt(d_qkv, ups) * adapter_columns(tokens, ups.shape[0])).astype(BF16)
    grads_ref[:, :width] = mm_tn(back, normed_ref[...])
    grads_ref[:, width:] = mm_tn(low_ref[...], d_qkv)
    blocks = grads_ref.shape[1] // LANES
    rank = grads_ref.shape[0] // count
    row = lax.broadcasted_iota(jnp.int32, (count, LANES), 0)
    ids = jnp.zeros((count, LANES), F32)
    per = region_ref.shape[2]
    for w in range(count):
        ids = jnp.where(row == w, region_ref[w // per, 0, w % per].astype(F32), ids)
    for b in range(blocks):
        cols = slice(b * LANES, (b + 1) * LANES)
        for r in range(rank):
            own = [grads_ref[w * rank + r : w * rank + r + 1, cols] for w in range(count)]
            tile = jnp.concatenate(own + [ids], axis=0)
            terms_ref[r * blocks + b] = tile.astype(terms_ref.dtype)


def reduce_kernel(terms_ref, sums_ref):
    _, pieces, regions, _ = sums_ref.shape
    devices, _, height, _ = terms_ref.shape
    for p in range(pieces):
        tile = terms_ref[:, p].astype(F32).reshape(devices * height, LANES)
        ids = pltpu.roll(tile, devices * height - height // 2, 0)
        row = lax.broadcasted_iota(jnp.int32, tile.shape, 0) % height
        lane = lax.broadcasted_iota(jnp.int32, tile.shape, 1).astype(F32)
        hot = jnp.where((ids == lane) & (row < height // 2), 1.0, 0.0).astype(BF16)
        sums = mm_tn(hot, tile.astype(BF16))[:regions].astype(sums_ref.dtype)
        for d in range(sums_ref.shape[0]):
            sums_ref[d, p] = sums


def scale_kernel(near_ref, far_ref, down_ref, up_ref, all_ref):
    regions, _, width = down_ref.shape
    rank, blocks = all_ref.shape[:2]
    outer, inner = near_ref.shape[:2]
    core = lax.axis_index("lat") % 2
    total = jnp.zeros((regions, LANES), F32)
    for side, ref in enumerate((near_ref, far_ref)):
        which = core if side == 0 else 1 - core
        for a in range(outer):
            for r in range(inner):
                for b in range(blocks):
                    part = ref[a, r, b].astype(F32)
                    total += part * part
                    all_ref[(a * 2 + which) * inner + r, b] = part
    size = rank * blocks * regions * LANES
    total = jnp.sum(jnp.sum(total, axis=0, keepdims=True), axis=1, keepdims=True)
    factor = lax.rsqrt(total * (1.0 / size) + 1e-06)
    for b in range(blocks):
        part = jnp.swapaxes(all_ref[:, b] * factor, 0, 1)
        start = b * LANES
        if start < width:
            down_ref[:, :, start : start + LANES] = part
        else:
            up_ref[:, :, start - width : start - width + LANES] = part


SMEM = pl.BlockSpec(memory_space=pltpu.SMEM)
VMEM = pl.BlockSpec(memory_space=pltpu.VMEM)


def call(kernel, places, outs, scratch=(), flops=0, moved=0, mib=32, name=None):
    return pl.pallas_call(
        kernel,
        in_specs=places,
        out_shape=outs,
        scratch_shapes=[pltpu.VMEM(dims, dtype) for dims, dtype in scratch],
        compiler_params=pltpu.CompilerParams(vmem_limit_bytes=mib * 1024 * 1024),
        cost_estimate=pl.CostEstimate(flops=flops, bytes_accessed=moved, transcendentals=0),
        name=name,
    )


def shape(*dims, dtype=F32):
    return jax.ShapeDtypeStruct(dims, dtype)


def move(array, step):
    lats, lons = lax.axis_size("lat"), lax.axis_size("lon")

    def index(a, b):
        return (a % lats) * lons + b % lons

    pairs = [
        (index(a, b), index(a + step[0], b + step[1])) for a in range(lats) for b in range(lons)
    ]
    return lax.ppermute(array, ("lat", "lon"), pairs)


def halos(field):
    return (
        field[:, :HALF_LAT, HALF_LON:],
        field[:, HALF_LAT:, :HALF_LON],
        field[:, :HALF_LAT, :HALF_LON],
    )


def move_halos(parts):
    south, east, corner = parts
    corner, east = move(corner, (-1, -1)), move(east, (0, -1))
    return move(south, (-1, 0)), east, corner


def local(
    pixels,
    land_patch_mask,
    region,
    patch_embed_weight,
    patch_embed_bias,
    land_embedding_vector,
    attention_norm_gain,
    query_key_value_weight,
    region_down_factor,
    region_up_factor,
    head_logit_scale,
    attention_output_weight,
    feedforward_gain,
    feedforward_up_weight,
    feedforward_down_weight,
    cotangent,
):
    levels, rows, cols, patch_len = pixels.shape
    width = patch_embed_weight.shape[1]
    inner = feedforward_up_weight.shape[1]
    regions, rank, _ = region_down_factor.shape
    count = region.size
    tokens = count * TOKENS
    groups = width // LANES
    devices = lax.axis_size("lat") * lax.axis_size("lon")

    wide = (levels, HALF_LAT, cols - HALF_LON, width)
    narrow = (levels, HALF_LAT, HALF_LON, width)
    pix_own, *pix = call(
        pack_kernel,
        [VMEM] * 2,
        tuple(shape(*dims, dtype=BF16) for dims in (wide, wide, narrow, narrow)),
        moved=2_000_000,
        name="pack_pixels",
    )(pixels, land_patch_mask)
    pix, cotangent = lax.optimization_barrier((pix, cotangent))
    pix = move_halos(pix)
    cot_own = cotangent[:, HALF_LAT:, HALF_LON:].astype(BF16)
    cot = move_halos(tuple(part.astype(BF16) for part in halos(cotangent)))

    hidden, normed, low, qk, v, probs = call(
        attention_kernel,
        [SMEM] * 2 + [VMEM] * 12,
        (
            shape(tokens, width),
            shape(tokens, width, dtype=BF16),
            shape(tokens, rank * count, dtype=BF16),
            shape(tokens, 2 * width),
            shape(tokens, width, dtype=BF16),
            shape(count * groups, TOKENS, PER_GROUP * TOKENS, dtype=BF16),
        ),
        (
            ((tokens, width), F32),
            ((tokens, width), F32),
            ((tokens, width), BF16),
            ((tokens, width), BF16),
            ((rank * count, width), F32),
            ((rank * count, 3 * width), F32),
            ((levels // WLEV, TOKENS, PER_GROUP * TOKENS), F32),
        ),
        flops=2 * tokens * width * 6 * width,
        moved=20_000_000,
        name="attention_forward",
    )(
        region, head_logit_scale, pix_own, *pix, patch_embed_weight, patch_embed_bias[None],
        land_embedding_vector[None], attention_norm_gain[None], query_key_value_weight,
        region_down_factor, region_up_factor, attention_output_weight,
    )
    home, north, west, diagonal, d_att = call(
        feed_kernel,
        [VMEM] * 9,
        (
            shape(*wide),
            shape(*wide, dtype=BF16),
            shape(*narrow, dtype=BF16),
            shape(*narrow, dtype=BF16),
            shape(tokens, width, dtype=BF16),
        ),
        (((tokens, width), F32),) * 3,
        flops=2 * tokens * width * 4 * inner,
        moved=20_000_000,
        name="feed_forward",
    )(
        hidden, cot_own, *cot, feedforward_gain[None], feedforward_up_weight, feedforward_down_weight,
        attention_output_weight,
    )
    diagonal, west, north = move(diagonal, (1, 1)), move(west, (0, 1)), move(north, (1, 0))
    pieces = rank * 4 * width // LANES
    terms = call(
        backward_kernel,
        [SMEM] * 2 + [VMEM] * 7,
        shape(pieces, 2 * count, LANES, dtype=BF16),
        (
            ((tokens, width), F32),
            ((tokens, width), BF16),
            ((tokens, width), F32),
            ((tokens, width), F32),
            ((tokens, 3 * width), BF16),
            ((rank * count, 3 * width), F32),
            ((rank * count, 4 * width), F32),
        ),
        flops=2 * tokens * width * 4 * width,
        moved=12_000_000,
        name="attention_backward",
    )(region, head_logit_scale, normed, low, qk, v, probs, d_att, region_up_factor)
    terms, north, west, diagonal = lax.optimization_barrier((terms, north, west, diagonal))
    upper = jnp.concatenate((diagonal, north), axis=2).astype(F32)
    lower = jnp.concatenate((west.astype(F32), home), axis=2)
    mixed_state = jnp.concatenate((upper, lower), axis=1)

    each = pieces // devices
    terms = lax.all_to_all(terms, AXES, 0, 0, tiled=True)
    sums = call(
        reduce_kernel,
        [VMEM],
        shape(devices // 2, each, regions, LANES, dtype=BF16),
        name="sum_by_region",
    )(terms.reshape(devices, each, 2 * count, LANES))
    lats, lons = lax.axis_size("lat"), lax.axis_size("lon")
    cores = [[a * lons + b for a in range(c, lats, 2) for b in range(lons)] for c in range(2)]
    near = lax.all_to_all(sums, AXES, 0, 0, axis_index_groups=cores, tiled=True)
    far = lax.ppermute(near, "lat", [(a, a ^ 1) for a in range(lats)])
    blocks = 4 * width // LANES
    order = (lats // 2, rank // lats, blocks, regions, LANES)
    step_down, step_up = call(
        scale_kernel,
        [VMEM] * 2,
        (shape(regions, rank, width), shape(regions, rank, 3 * width)),
        (((rank, blocks, regions, LANES), F32),),
        name="scale_steps",
    )(near.reshape(order), far.reshape(order))
    return (mixed_state, step_down, step_up)


def solution(mesh):
    field = P(None, "lat", "lon", None)
    placed = (field, P("lat", "lon"), P(None, "lat", "lon")) + (P(),) * 12 + (field,)
    return jax.shard_map(
        local, mesh=mesh, in_specs=placed, out_specs=(field, P(), P()), check_vma=False
    )
```

```python
import jax
import jax.numpy as jnp
from jax import lax
from jax.experimental import pallas as pl
from jax.experimental.pallas import tpu as pltpu
from jax.sharding import PartitionSpec as P

WLEV = 2
WLAT = 6
WLON = 12
TOKENS = WLEV * WLAT * WLON
HALF_LAT = WLAT // 2
HALF_LON = WLON // 2
LANES = 128
HEAD = 32
PER_GROUP = LANES // HEAD

AXES = ("lat", "lon")
LOG2_E = 1.4426950408889634
F32 = jnp.float32
BF16 = jnp.bfloat16


def mm(a, b):
    return lax.dot_general(a, b, (((1,), (0,)), ((), ())), preferred_element_type=F32)


def mm_nt(a, b):
    return lax.dot_general(a, b, (((1,), (1,)), ((), ())), preferred_element_type=F32)


def mm_tn(a, b):
    return lax.dot_general(a, b, (((0,), (0,)), ((), ())), preferred_element_type=F32)


def head_mean(values):
    wide = 2 * LANES
    rows = lax.broadcasted_iota(jnp.int32, (wide, wide), 0) // HEAD
    cols = lax.broadcasted_iota(jnp.int32, (wide, wide), 1) // HEAD
    block = jnp.where(rows == cols, 1.0 / HEAD, 0.0).astype(BF16)
    parts = []
    for start in range(0, values.shape[1], wide):
        part = values[:, start : start + wide]
        top = part.astype(BF16)
        rest = (part - top.astype(F32)).astype(BF16)
        parts.append(mm(top, block) + mm(rest, block))
    return jnp.concatenate(parts, axis=1)


def head_masks(dtype):
    lane = lax.broadcasted_iota(jnp.int32, (1, LANES), 1) // HEAD
    return [jnp.where(lane == h, 1.0, 0.0).astype(dtype) for h in range(PER_GROUP)]


def stack_heads(x, masks):
    return jnp.concatenate([x * m for m in masks], axis=0)


def unstack_heads(x, masks):
    tokens = x.shape[0] // PER_GROUP
    return sum(x[h * tokens : (h + 1) * tokens] * m for h, m in enumerate(masks))


def adapter_columns(tokens, columns):
    rank = columns // (tokens // TOKENS)
    own = lax.broadcasted_iota(jnp.int32, (tokens, columns), 0)
    first = lax.broadcasted_iota(jnp.int32, (tokens, columns), 1) // rank * TOKENS
    return jnp.where((own >= first) & (own < first + TOKENS), 1.0, 0.0)


def factors(region_ref, factor_ref, all_ref):
    rank = factor_ref.shape[1]
    ids = [region_ref[a, 0, b] for a in range(region_ref.shape[0]) for b in range(region_ref.shape[2])]
    for w, r in enumerate(ids):
        all_ref[w * rank : (w + 1) * rank, :] = factor_ref[r].astype(F32)
    return all_ref[...].astype(BF16)


def scale_row(scale_ref, width):
    head = lax.broadcasted_iota(jnp.int32, (1, width), 1) // HEAD
    row = jnp.zeros((1, width), F32)
    for h in range(width // HEAD):
        row = jnp.where(head == h, scale_ref[h] / HEAD, row)
    return row


def same_group(level, south):
    def group(token):
        late = jnp.where(token >= TOKENS // WLEV, 1, 0) * level
        low = jnp.where(token // WLON % WLAT >= HALF_LAT, 1, 0) * south
        return 2 * late + low

    keys = lax.broadcasted_iota(jnp.int32, (TOKENS, 1), 0)
    queries = lax.broadcasted_iota(jnp.int32, (1, PER_GROUP * TOKENS), 1) % TOKENS
    return jnp.where(group(keys) == group(queries), 1.0, 0.0)


def pieces_of(shape):
    levels, _, cols, _ = shape
    across = (cols + HALF_LON) // WLON
    for level in range(levels):
        for row in range(WLAT):
            within = level % WLEV * WLAT * WLON + row * WLON
            starts = [((level // WLEV) * across + b) * TOKENS + within for b in range(across)]
            yield (level + WLEV // 2) % levels, row // HALF_LAT, row % HALF_LAT, starts


def into_windows(stage_ref, own_ref, south_ref, east_ref, corner_ref):
    for level, half, row, starts in pieces_of(own_ref.shape):
        wide = (south_ref if half else own_ref)[level, row].astype(F32)
        narrow = (corner_ref if half else east_ref)[level, row].astype(F32)
        for b, start in enumerate(starts[:-1]):
            stage_ref[start : start + WLON, :] = wide[b * WLON : (b + 1) * WLON]
        start = starts[-1]
        stage_ref[start : start + HALF_LON, :] = wide[-HALF_LON:]
        stage_ref[start + HALF_LON : start + WLON, :] = narrow


def out_of_windows(stage_ref, own_ref, north_ref, west_ref, corner_ref):
    for level, half, row, starts in pieces_of(own_ref.shape):
        wide = [stage_ref[start : start + WLON, :] for start in starts[:-1]]
        start = starts[-1]
        wide.append(stage_ref[start : start + HALF_LON, :])
        narrow = stage_ref[start + HALF_LON : start + WLON, :]
        wide_ref, narrow_ref = (north_ref, corner_ref) if half else (own_ref, west_ref)
        wide_ref[level, row] = jnp.concatenate(wide, axis=0).astype(wide_ref.dtype)
        narrow_ref[level, row] = narrow.astype(narrow_ref.dtype)


def norm_stats(x):
    width = x.shape[1]
    mean = jnp.sum(x, axis=1, keepdims=True) * (1.0 / width)
    centred = x - mean
    spread = jnp.sum(centred * centred, axis=1, keepdims=True) * (1.0 / width)
    return centred, lax.rsqrt(spread + 1e-05)


def gelu_and_slope(u):
    t = 1.0 / (1.0 + (0.3275911 * 0.5**0.5) * jnp.abs(u))
    e = jnp.exp2((-0.5 * LOG2_E) * (u * u))
    poly = 0.5 * 1.061405429
    for c in (-1.453152027, 1.421413741, -0.284496736, 0.254829592):
        poly = poly * t + 0.5 * c
    tail = poly * t * e
    phi = jnp.where(u < 0, tail, 1.0 - tail)
    return u * phi, phi + (0.3989422804014327 * u) * e


def pack_kernel(pixels_ref, land_ref, own_ref, south_ref, east_ref, corner_ref):
    levels, rows, cols, patch_len = pixels_ref.shape
    width = own_ref.shape[3]
    eye = lax.broadcasted_iota(jnp.int32, (cols, cols), 0)
    eye = jnp.where(eye == lax.broadcasted_iota(jnp.int32, (cols, cols), 1), 1.0, 0.0)
    land = mm_nt(eye.astype(BF16), land_ref[...].astype(F32).astype(BF16))
    lane = lax.broadcasted_iota(jnp.int32, (cols, width), 1)
    blank = jnp.zeros((cols, width - patch_len), F32)
    for level in range(levels):
        for row in range(rows):
            patch = jnp.concatenate((pixels_ref[level, row].astype(F32), blank), axis=1)
            patch = jnp.where(lane == patch_len, land[:, row : row + 1], patch).astype(BF16)
            half, at = divmod(row, HALF_LAT)
            (own_ref if half else south_ref)[level, at] = patch[HALF_LON:]
            (east_ref if half else corner_ref)[level, at] = patch[:HALF_LON]


def attention_kernel(
    region_ref, temper_ref, own_ref, south_ref, east_ref, corner_ref, wp_ref, bias_ref, land_ref,
    gain_ref, wqkv_ref, down_ref, up_ref, wo_ref,
    hidden_ref, normed_ref, low_ref, inv_ref, qs_ref, kn_ref, v_ref, probs_ref,
    state_ref, att_ref, downs_ref, ups_ref, same_ref,
):
    tokens, width = state_ref.shape
    count = tokens // TOKENS
    groups = width // LANES
    masks, narrow_masks = head_masks(F32), head_masks(BF16)
    patch_len = wp_ref.shape[0]
    into_windows(state_ref, own_ref, south_ref, east_ref, corner_ref)
    pix = state_ref[:, :patch_len].astype(BF16)
    land = state_ref[:, patch_len : patch_len + 1]
    state = mm(pix, wp_ref[...]) + bias_ref[...] + land * land_ref[...]
    state_ref[...] = state
    centred, inv = norm_stats(state)
    normed = (centred * inv * gain_ref[...]).astype(BF16)
    normed_ref[...] = normed
    downs = factors(region_ref, down_ref, downs_ref)
    ups = factors(region_ref, up_ref, ups_ref)
    low = (mm_nt(normed, downs) * adapter_columns(tokens, downs.shape[0])).astype(BF16)
    low_ref[...] = low
    scale = scale_row(temper_ref, width)
    for part in range(3):
        cols = slice(part * width, (part + 1) * width)
        qkv = mm(normed, wqkv_ref[:, cols]) + mm(low, ups[:, cols])
        if part == 2:
            v_ref[...] = qkv.astype(BF16)
        else:
            inv = lax.rsqrt(head_mean(qkv * qkv) + 1e-06)
            inv_ref[:, cols] = inv
            if part == 0:
                qs_ref[...] = (qkv * inv * (scale * LOG2_E)).astype(BF16)
            else:
                kn_ref[...] = (qkv * inv).astype(BF16)
    last_band = lax.axis_index("lat") == lax.axis_size("lat") - 1
    south = jnp.where(last_band, 1, 0).astype(jnp.int32)
    parts = same_ref.shape[0]
    for part in range(parts):
        same_ref[part] = same_group(1 if part == parts - 1 else 0, south)

    def window(w, carry):
        rows = pl.ds(pl.multiple_of(w * TOKENS, TOKENS), TOKENS)
        same = same_ref[w // (count // parts)]
        for g in range(groups):
            cols = slice(g * LANES, (g + 1) * LANES)
            stack = stack_heads(qs_ref[rows, cols], narrow_masks)
            weights = jnp.exp2(mm_nt(kn_ref[rows, cols], stack)) * same
            total = jnp.sum(weights, axis=0, keepdims=True)
            probs = (weights * (1.0 / total)).astype(BF16)
            probs_ref[w * groups + g] = probs
            mixed = mm_tn(probs, v_ref[rows, cols])
            att_ref[rows, cols] = unstack_heads(mixed, masks).astype(BF16)
        return carry

    lax.fori_loop(0, count, window, 0, unroll=True)
    z = mm(att_ref[...], wo_ref[...]).astype(BF16)
    hidden_ref[...] = state_ref[...] + z.astype(F32)


def feed_kernel(
    hidden_ref, own_ref, south_ref, east_ref, corner_ref, gain_ref, wup_ref, wdn_ref, wo_ref,
    home_ref, north_ref, west_ref, diagonal_ref, datt_ref,
    cot_ref, mixed_ref, unit_ref,
):
    tokens, width = hidden_ref.shape
    into_windows(cot_ref, own_ref, south_ref, east_ref, corner_ref)
    hidden = hidden_ref[...]
    centred, inv = norm_stats(hidden)
    unit = centred * inv
    normed = (unit * gain_ref[...]).astype(BF16)
    cot = cot_ref[...].astype(BF16)
    mixed_ref[...] = hidden
    unit_ref[...] = unit
    d_normed = jnp.zeros((tokens, width), F32)
    chunk = 2048
    for c in range(wup_ref.shape[1] // chunk):
        cols = slice(c * chunk, (c + 1) * chunk)
        act, slope = gelu_and_slope(mm(normed, wup_ref[:, cols]))
        mixed_ref[...] += mm(act.astype(BF16), wdn_ref[cols, :])
        d_up = mm_nt(cot, wdn_ref[cols, :]) * slope
        d_normed += mm_nt(d_up.astype(BF16), wup_ref[:, cols])
    out_of_windows(mixed_ref, home_ref, north_ref, west_ref, diagonal_ref)
    d_unit = d_normed * gain_ref[...]
    unit = unit_ref[...]
    first = jnp.sum(d_unit, axis=1, keepdims=True) * (1.0 / width)
    second = jnp.sum(d_unit * unit, axis=1, keepdims=True) * (1.0 / width)
    d_hidden = cot_ref[...] + inv * (d_unit - first - unit * second)
    datt_ref[...] = mm_nt(d_hidden.astype(BF16), wo_ref[...]).astype(BF16)


def backward_kernel(
    region_ref, temper_ref, normed_ref, low_ref, inv_ref, qs_ref, kn_ref, v_ref, probs_ref, datt_ref,
    up_ref,
    terms_ref,
    dq_ref, dk_ref, dqkv_ref, ups_ref, grads_ref,
):
    tokens, width = normed_ref.shape
    count = tokens // TOKENS
    groups = width // LANES
    masks, narrow_masks = head_masks(F32), head_masks(BF16)
    scale = scale_row(temper_ref, width)

    def window(w, carry):
        rows = pl.ds(pl.multiple_of(w * TOKENS, TOKENS), TOKENS)
        for g in range(groups):
            cols = slice(g * LANES, (g + 1) * LANES)
            d_stack = stack_heads(datt_ref[rows, cols], narrow_masks)
            q_stack = stack_heads(qs_ref[rows, cols], narrow_masks)
            probs = probs_ref[w * groups + g]
            d_probs = mm_nt(v_ref[rows, cols], d_stack)
            wide = probs.astype(F32)
            prod = wide * d_probs
            d_scores = (prod - wide * jnp.sum(prod, axis=0, keepdims=True)).astype(BF16)
            dqkv_ref[rows, slice(2 * width + g * LANES, 2 * width + (g + 1) * LANES)] = mm(
                probs, d_stack
            ).astype(BF16)
            dk_ref[rows, cols] = mm(d_scores, q_stack)
            dq_ref[rows, cols] = unstack_heads(mm_tn(d_scores, kn_ref[rows, cols]), masks)
        return carry

    lax.fori_loop(0, count, window, 0, unroll=True)
    scales = ((scale, 1.0 / (scale * (LOG2_E * LOG2_E))), (1.0 / LOG2_E, 1.0 / LOG2_E))
    for part, (unit_ref, grad_ref) in enumerate(((qs_ref, dq_ref), (kn_ref, dk_ref))):
        cols = slice(part * width, (part + 1) * width)
        unit, grad = unit_ref[...].astype(F32), grad_ref[...]
        along = unit * head_mean(grad * unit)
        first, second = scales[part]
        dqkv_ref[:, cols] = (inv_ref[:, cols] * (grad * first - along * second)).astype(BF16)
    ups = factors(region_ref, up_ref, ups_ref)
    d_qkv = dqkv_ref[...]
    back = (mm_nt(d_qkv, ups) * adapter_columns(tokens, ups.shape[0])).astype(BF16)
    grads_ref[:, :width] = mm_tn(back, normed_ref[...])
    grads_ref[:, width:] = mm_tn(low_ref[...], d_qkv)
    blocks = grads_ref.shape[1] // LANES
    rank = grads_ref.shape[0] // count
    row = lax.broadcasted_iota(jnp.int32, (count, LANES), 0)
    ids = jnp.zeros((count, LANES), F32)
    per = region_ref.shape[2]
    for w in range(count):
        ids = jnp.where(row == w, region_ref[w // per, 0, w % per].astype(F32), ids)
    for b in range(blocks):
        cols = slice(b * LANES, (b + 1) * LANES)
        for r in range(rank):
            own = [grads_ref[w * rank + r : w * rank + r + 1, cols] for w in range(count)]
            tile = jnp.concatenate(own + [ids], axis=0)
            terms_ref[r * blocks + b] = tile.astype(terms_ref.dtype)


def reduce_kernel(terms_ref, sums_ref):
    _, pieces, regions, _ = sums_ref.shape
    devices, _, height, _ = terms_ref.shape
    for p in range(pieces):
        tile = terms_ref[:, p].astype(F32).reshape(devices * height, LANES)
        ids = pltpu.roll(tile, devices * height - height // 2, 0)
        row = lax.broadcasted_iota(jnp.int32, tile.shape, 0) % height
        lane = lax.broadcasted_iota(jnp.int32, tile.shape, 1).astype(F32)
        hot = jnp.where((ids == lane) & (row < height // 2), 1.0, 0.0).astype(BF16)
        sums = mm_tn(hot, tile.astype(BF16))[:regions].astype(sums_ref.dtype)
        for d in range(sums_ref.shape[0]):
            sums_ref[d, p] = sums


def scale_kernel(near_ref, far_ref, down_ref, up_ref, all_ref):
    regions, _, width = down_ref.shape
    rank, blocks = all_ref.shape[:2]
    outer, inner = near_ref.shape[:2]
    core = lax.axis_index("lat") % 2
    total = jnp.zeros((regions, LANES), F32)
    for side, ref in enumerate((near_ref, far_ref)):
        which = core if side == 0 else 1 - core
        for a in range(outer):
            for r in range(inner):
                for b in range(blocks):
                    part = ref[a, r, b].astype(F32)
                    total += part * part
                    all_ref[(a * 2 + which) * inner + r, b] = part
    size = rank * blocks * regions * LANES
    total = jnp.sum(jnp.sum(total, axis=0, keepdims=True), axis=1, keepdims=True)
    factor = lax.rsqrt(total * (1.0 / size) + 1e-06)
    for b in range(blocks):
        part = jnp.swapaxes(all_ref[:, b] * factor, 0, 1)
        start = b * LANES
        if start < width:
            down_ref[:, :, start : start + LANES] = part
        else:
            up_ref[:, :, start - width : start - width + LANES] = part


SMEM = pl.BlockSpec(memory_space=pltpu.SMEM)
VMEM = pl.BlockSpec(memory_space=pltpu.VMEM)


def call(kernel, places, outs, scratch=(), flops=0, moved=0, mib=32, name=None):
    return pl.pallas_call(
        kernel,
        in_specs=places,
        out_shape=outs,
        scratch_shapes=[pltpu.VMEM(dims, dtype) for dims, dtype in scratch],
        compiler_params=pltpu.CompilerParams(vmem_limit_bytes=mib * 1024 * 1024),
        cost_estimate=pl.CostEstimate(flops=flops, bytes_accessed=moved, transcendentals=0),
        name=name,
    )


def shape(*dims, dtype=F32):
    return jax.ShapeDtypeStruct(dims, dtype)


def move(array, step):
    lats, lons = lax.axis_size("lat"), lax.axis_size("lon")

    def index(a, b):
        return (a % lats) * lons + b % lons

    pairs = [
        (index(a, b), index(a + step[0], b + step[1])) for a in range(lats) for b in range(lons)
    ]
    return lax.ppermute(array, ("lat", "lon"), pairs)


def halos(field):
    return (
        field[:, :HALF_LAT, HALF_LON:],
        field[:, HALF_LAT:, :HALF_LON],
        field[:, :HALF_LAT, :HALF_LON],
    )


def move_halos(parts):
    south, east, corner = parts
    corner, east = move(corner, (-1, -1)), move(east, (0, -1))
    return move(south, (-1, 0)), east, corner


def local(
    pixels,
    land_patch_mask,
    region,
    patch_embed_weight,
    patch_embed_bias,
    land_embedding_vector,
    attention_norm_gain,
    query_key_value_weight,
    region_down_factor,
    region_up_factor,
    head_logit_scale,
    attention_output_weight,
    feedforward_gain,
    feedforward_up_weight,
    feedforward_down_weight,
    cotangent,
):
    levels, rows, cols, patch_len = pixels.shape
    width = patch_embed_weight.shape[1]
    inner = feedforward_up_weight.shape[1]
    regions, rank, _ = region_down_factor.shape
    count = region.size
    tokens = count * TOKENS
    groups = width // LANES
    devices = lax.axis_size("lat") * lax.axis_size("lon")

    wide = (levels, HALF_LAT, cols - HALF_LON, width)
    narrow = (levels, HALF_LAT, HALF_LON, width)
    pix_own, *pix = call(
        pack_kernel,
        [VMEM] * 2,
        tuple(shape(*dims, dtype=BF16) for dims in (wide, wide, narrow, narrow)),
        moved=2_000_000,
        name="pack_pixels",
    )(pixels, land_patch_mask)
    pix, cotangent = lax.optimization_barrier((pix, cotangent))
    pix = move_halos(pix)
    cot_own = cotangent[:, HALF_LAT:, HALF_LON:].astype(BF16)
    cot = move_halos(tuple(part.astype(BF16) for part in halos(cotangent)))

    hidden, normed, low, inv, qs, kn, v, probs = call(
        attention_kernel,
        [SMEM] * 2 + [VMEM] * 12,
        (
            shape(tokens, width),
            shape(tokens, width, dtype=BF16),
            shape(tokens, rank * count, dtype=BF16),
            shape(tokens, 2 * width),
            shape(tokens, width, dtype=BF16),
            shape(tokens, width, dtype=BF16),
            shape(tokens, width, dtype=BF16),
            shape(count * groups, TOKENS, PER_GROUP * TOKENS, dtype=BF16),
        ),
        (
            ((tokens, width), F32),
            ((tokens, width), BF16),
            ((rank * count, width), F32),
            ((rank * count, 3 * width), F32),
            ((levels // WLEV, TOKENS, PER_GROUP * TOKENS), F32),
        ),
        flops=2 * tokens * width * 6 * width,
        moved=20_000_000,
        name="attention_forward",
    )(
        region, head_logit_scale, pix_own, *pix, patch_embed_weight, patch_embed_bias[None],
        land_embedding_vector[None], attention_norm_gain[None], query_key_value_weight,
        region_down_factor, region_up_factor, attention_output_weight,
    )
    home, north, west, diagonal, d_att = call(
        feed_kernel,
        [VMEM] * 9,
        (
            shape(*wide),
            shape(*wide, dtype=BF16),
            shape(*narrow, dtype=BF16),
            shape(*narrow, dtype=BF16),
            shape(tokens, width, dtype=BF16),
        ),
        (((tokens, width), F32),) * 3,
        flops=2 * tokens * width * 4 * inner,
        moved=20_000_000,
        name="feed_forward",
    )(
        hidden, cot_own, *cot, feedforward_gain[None], feedforward_up_weight, feedforward_down_weight,
        attention_output_weight,
    )
    pieces = rank * 4 * width // LANES
    terms = call(
        backward_kernel,
        [SMEM] * 2 + [VMEM] * 9,
        shape(pieces, 2 * count, LANES, dtype=BF16),
        (
            ((tokens, width), F32),
            ((tokens, width), F32),
            ((tokens, 3 * width), BF16),
            ((rank * count, 3 * width), F32),
            ((rank * count, 4 * width), F32),
        ),
        flops=2 * tokens * width * 4 * width,
        moved=12_000_000,
        name="attention_backward",
    )(
        region, head_logit_scale, normed, low, inv, qs, kn, v, probs, d_att, region_up_factor
    )
    each = pieces // devices
    terms = lax.all_to_all(terms, AXES, 0, 0, tiled=True)
    sums = call(
        reduce_kernel,
        [VMEM],
        shape(devices // 2, each, regions, LANES, dtype=BF16),
        name="sum_by_region",
    )(terms.reshape(devices, each, 2 * count, LANES))
    lats, lons = lax.axis_size("lat"), lax.axis_size("lon")
    cores = [[a * lons + b for a in range(c, lats, 2) for b in range(lons)] for c in range(2)]
    sums, diagonal, west, north = lax.optimization_barrier((sums, diagonal, west, north))
    near = lax.all_to_all(sums, AXES, 0, 0, axis_index_groups=cores, tiled=True)
    diagonal, west, north = move(diagonal, (1, 1)), move(west, (0, 1)), move(north, (1, 0))
    near, diagonal, west, north = lax.optimization_barrier((near, diagonal, west, north))
    upper = jnp.concatenate((diagonal, north), axis=2).astype(F32)
    lower = jnp.concatenate((west.astype(F32), home), axis=2)
    mixed_state = jnp.concatenate((upper, lower), axis=1)
    far = lax.ppermute(near, "lat", [(a, a ^ 1) for a in range(lats)])
    blocks = 4 * width // LANES
    order = (lats // 2, rank // lats, blocks, regions, LANES)
    step_down, step_up = call(
        scale_kernel,
        [VMEM] * 2,
        (shape(regions, rank, width), shape(regions, rank, 3 * width)),
        (((rank, blocks, regions, LANES), F32),),
        name="scale_steps",
    )(near.reshape(order), far.reshape(order))
    return (mixed_state, step_down, step_up)


def solution(mesh):
    field = P(None, "lat", "lon", None)
    placed = (field, P("lat", "lon"), P(None, "lat", "lon")) + (P(),) * 12 + (field,)
    return jax.shard_map(
        local, mesh=mesh, in_specs=placed, out_specs=(field, P(), P()), check_vma=False
    )
```

```python
import jax
import jax.numpy as jnp
from jax import lax
from jax.experimental import pallas as pl
from jax.experimental.pallas import tpu as pltpu
from jax.sharding import PartitionSpec as P

WLEV = 2
WLAT = 6
WLON = 12
TOKENS = WLEV * WLAT * WLON
HALF_LAT = WLAT // 2
HALF_LON = WLON // 2
LANES = 128
HEAD = 32
PER_GROUP = LANES // HEAD

AXES = ("lat", "lon")
LOG2_E = 1.4426950408889634
F32 = jnp.float32
BF16 = jnp.bfloat16


def mm(a, b):
    return lax.dot_general(a, b, (((1,), (0,)), ((), ())), preferred_element_type=F32)


def mm_nt(a, b):
    return lax.dot_general(a, b, (((1,), (1,)), ((), ())), preferred_element_type=F32)


def mm_tn(a, b):
    return lax.dot_general(a, b, (((0,), (0,)), ((), ())), preferred_element_type=F32)


def head_mean(values):
    wide = 2 * LANES
    rows = lax.broadcasted_iota(jnp.int32, (wide, wide), 0) // HEAD
    cols = lax.broadcasted_iota(jnp.int32, (wide, wide), 1) // HEAD
    block = jnp.where(rows == cols, 1.0 / HEAD, 0.0).astype(BF16)
    parts = []
    for start in range(0, values.shape[1], wide):
        part = values[:, start : start + wide]
        top = part.astype(BF16)
        rest = (part - top.astype(F32)).astype(BF16)
        parts.append(mm(top, block) + mm(rest, block))
    return jnp.concatenate(parts, axis=1)


def head_masks(dtype):
    lane = lax.broadcasted_iota(jnp.int32, (1, LANES), 1) // HEAD
    return [jnp.where(lane == h, 1.0, 0.0).astype(dtype) for h in range(PER_GROUP)]


def stack_heads(x, masks):
    return jnp.concatenate([x * m for m in masks], axis=0)


def unstack_heads(x, masks):
    tokens = x.shape[0] // PER_GROUP
    return sum(x[h * tokens : (h + 1) * tokens] * m for h, m in enumerate(masks))


def adapter_columns(tokens, columns):
    rank = columns // (tokens // TOKENS)
    own = lax.broadcasted_iota(jnp.int32, (tokens, columns), 0)
    first = lax.broadcasted_iota(jnp.int32, (tokens, columns), 1) // rank * TOKENS
    return jnp.where((own >= first) & (own < first + TOKENS), 1.0, 0.0)


def factors(region_ref, factor_ref, all_ref):
    rank = factor_ref.shape[1]
    ids = [region_ref[a, 0, b] for a in range(region_ref.shape[0]) for b in range(region_ref.shape[2])]
    for w, r in enumerate(ids):
        all_ref[w * rank : (w + 1) * rank, :] = factor_ref[r].astype(F32)
    return all_ref[...].astype(BF16)


def scale_row(scale_ref, width):
    head = lax.broadcasted_iota(jnp.int32, (1, width), 1) // HEAD
    row = jnp.zeros((1, width), F32)
    for h in range(width // HEAD):
        row = jnp.where(head == h, scale_ref[h] / HEAD, row)
    return row


def same_group(level, south):
    def group(token):
        late = jnp.where(token >= TOKENS // WLEV, 1, 0) * level
        low = jnp.where(token // WLON % WLAT >= HALF_LAT, 1, 0) * south
        return 2 * late + low

    keys = lax.broadcasted_iota(jnp.int32, (TOKENS, 1), 0)
    queries = lax.broadcasted_iota(jnp.int32, (1, PER_GROUP * TOKENS), 1) % TOKENS
    return jnp.where(group(keys) == group(queries), 1.0, 0.0)


def pieces_of(shape):
    levels, _, cols, _ = shape
    across = (cols + HALF_LON) // WLON
    for level in range(levels):
        for row in range(WLAT):
            within = level % WLEV * WLAT * WLON + row * WLON
            starts = [((level // WLEV) * across + b) * TOKENS + within for b in range(across)]
            yield (level + WLEV // 2) % levels, row // HALF_LAT, row % HALF_LAT, starts


def into_windows(stage_ref, own_ref, south_ref, east_ref, corner_ref):
    for level, half, row, starts in pieces_of(own_ref.shape):
        wide = (south_ref if half else own_ref)[level, row].astype(F32)
        narrow = (corner_ref if half else east_ref)[level, row].astype(F32)
        for b, start in enumerate(starts[:-1]):
            stage_ref[start : start + WLON, :] = wide[b * WLON : (b + 1) * WLON]
        start = starts[-1]
        stage_ref[start : start + HALF_LON, :] = wide[-HALF_LON:]
        stage_ref[start + HALF_LON : start + WLON, :] = narrow


def out_of_windows(stage_ref, own_ref, north_ref, west_ref, corner_ref):
    for level, half, row, starts in pieces_of(own_ref.shape):
        wide = [stage_ref[start : start + WLON, :] for start in starts[:-1]]
        start = starts[-1]
        wide.append(stage_ref[start : start + HALF_LON, :])
        narrow = stage_ref[start + HALF_LON : start + WLON, :]
        wide_ref, narrow_ref = (north_ref, corner_ref) if half else (own_ref, west_ref)
        wide_ref[level, row] = jnp.concatenate(wide, axis=0).astype(wide_ref.dtype)
        narrow_ref[level, row] = narrow.astype(narrow_ref.dtype)


def norm_stats(x):
    width = x.shape[1]
    mean = jnp.sum(x, axis=1, keepdims=True) * (1.0 / width)
    centred = x - mean
    spread = jnp.sum(centred * centred, axis=1, keepdims=True) * (1.0 / width)
    return centred, lax.rsqrt(spread + 1e-05)


def gelu_and_slope(u):
    phi = 0.5 + 0.5 * lax.erf(u * 0.5**0.5)
    return u * phi, phi + (0.3989422804014327 * u) * jnp.exp2((-0.5 * LOG2_E) * (u * u))


def pack_kernel(pixels_ref, land_ref, own_ref, south_ref, east_ref, corner_ref):
    levels, rows, cols, patch_len = pixels_ref.shape
    width = own_ref.shape[3]
    eye = lax.broadcasted_iota(jnp.int32, (cols, cols), 0)
    eye = jnp.where(eye == lax.broadcasted_iota(jnp.int32, (cols, cols), 1), 1.0, 0.0)
    land = mm_nt(eye.astype(BF16), land_ref[...])
    lane = lax.broadcasted_iota(jnp.int32, (cols, width), 1)
    blank = jnp.zeros((cols, width - patch_len), F32)
    for level in range(levels):
        for row in range(rows):
            patch = jnp.concatenate((pixels_ref[level, row].astype(F32), blank), axis=1)
            patch = jnp.where(lane == patch_len, land[:, row : row + 1], patch).astype(BF16)
            half, at = divmod(row, HALF_LAT)
            (own_ref if half else south_ref)[level, at] = patch[HALF_LON:]
            (east_ref if half else corner_ref)[level, at] = patch[:HALF_LON]


def attention_kernel(
    region_ref, temper_ref, own_ref, south_ref, east_ref, corner_ref, wp_ref, bias_ref, land_ref,
    gain_ref, wqkv_ref, down_ref, up_ref, wo_ref,
    hidden_ref, normed_ref, low_ref, inv_ref, qs_ref, kn_ref, v_ref, probs_ref,
    state_ref, att_ref, downs_ref, ups_ref, same_ref,
):
    tokens, width = state_ref.shape
    count = tokens // TOKENS
    groups = width // LANES
    masks, narrow_masks = head_masks(F32), head_masks(BF16)
    patch_len = wp_ref.shape[0]
    into_windows(state_ref, own_ref, south_ref, east_ref, corner_ref)
    pix = state_ref[:, :patch_len].astype(BF16)
    land = state_ref[:, patch_len : patch_len + 1]
    state = mm(pix, wp_ref[...]) + bias_ref[...] + land * land_ref[...]
    state_ref[...] = state
    centred, inv = norm_stats(state)
    normed = (centred * inv * gain_ref[...]).astype(BF16)
    normed_ref[...] = normed
    downs = factors(region_ref, down_ref, downs_ref)
    ups = factors(region_ref, up_ref, ups_ref)
    low = (mm_nt(normed, downs) * adapter_columns(tokens, downs.shape[0])).astype(BF16)
    low_ref[...] = low
    scale = scale_row(temper_ref, width)
    for part in range(3):
        cols = slice(part * width, (part + 1) * width)
        qkv = mm(normed, wqkv_ref[:, cols]) + mm(low, ups[:, cols])
        if part == 2:
            v_ref[...] = qkv.astype(BF16)
        else:
            inv = lax.rsqrt(head_mean(qkv * qkv) + 1e-06)
            inv_ref[:, cols] = inv
            if part == 0:
                qs_ref[...] = (qkv * inv * (scale * LOG2_E)).astype(BF16)
            else:
                kn_ref[...] = (qkv * inv).astype(BF16)
    last_band = lax.axis_index("lat") == lax.axis_size("lat") - 1
    south = jnp.where(last_band, 1, 0).astype(jnp.int32)
    parts = same_ref.shape[0]
    for part in range(parts):
        same_ref[part] = same_group(1 if part == parts - 1 else 0, south)

    def window(w, carry):
        rows = pl.ds(pl.multiple_of(w * TOKENS, TOKENS), TOKENS)
        same = same_ref[w // (count // parts)]
        for g in range(groups):
            cols = slice(g * LANES, (g + 1) * LANES)
            stack = stack_heads(qs_ref[rows, cols], narrow_masks)
            weights = jnp.exp2(mm_nt(kn_ref[rows, cols], stack)) * same
            total = jnp.sum(weights, axis=0, keepdims=True)
            probs = (weights * (1.0 / total)).astype(BF16)
            probs_ref[w * groups + g] = probs
            mixed = mm_tn(probs, v_ref[rows, cols])
            att_ref[rows, cols] = unstack_heads(mixed, masks).astype(BF16)
        return carry

    lax.fori_loop(0, count, window, 0, unroll=True)
    z = mm(att_ref[...], wo_ref[...]).astype(BF16)
    hidden_ref[...] = state_ref[...] + z.astype(F32)


def feed_kernel(
    hidden_ref, own_ref, south_ref, east_ref, corner_ref, gain_ref, wup_ref, wdn_ref, wo_ref,
    home_ref, north_ref, west_ref, diagonal_ref, datt_ref,
    cot_ref, mixed_ref, unit_ref,
):
    tokens, width = hidden_ref.shape
    into_windows(cot_ref, own_ref, south_ref, east_ref, corner_ref)
    hidden = hidden_ref[...]
    centred, inv = norm_stats(hidden)
    unit = centred * inv
    normed = (unit * gain_ref[...]).astype(BF16)
    cot = cot_ref[...].astype(BF16)
    mixed_ref[...] = hidden
    unit_ref[...] = unit
    d_normed = jnp.zeros((tokens, width), F32)
    chunk = 2048
    for c in range(wup_ref.shape[1] // chunk):
        cols = slice(c * chunk, (c + 1) * chunk)
        act, slope = gelu_and_slope(mm(normed, wup_ref[:, cols]))
        mixed_ref[...] += mm(act.astype(BF16), wdn_ref[cols, :])
        d_up = mm_nt(cot, wdn_ref[cols, :]) * slope
        d_normed += mm_nt(d_up.astype(BF16), wup_ref[:, cols])
    out_of_windows(mixed_ref, home_ref, north_ref, west_ref, diagonal_ref)
    d_unit = d_normed * gain_ref[...]
    unit = unit_ref[...]
    first = jnp.sum(d_unit, axis=1, keepdims=True) * (1.0 / width)
    second = jnp.sum(d_unit * unit, axis=1, keepdims=True) * (1.0 / width)
    d_hidden = cot_ref[...] + inv * (d_unit - first - unit * second)
    datt_ref[...] = mm_nt(d_hidden.astype(BF16), wo_ref[...]).astype(BF16)


def backward_kernel(
    region_ref, temper_ref, normed_ref, low_ref, inv_ref, qs_ref, kn_ref, v_ref, probs_ref, datt_ref,
    up_ref,
    terms_ref,
    dq_ref, dk_ref, dqkv_ref, ups_ref, grads_ref,
):
    tokens, width = normed_ref.shape
    count = tokens // TOKENS
    groups = width // LANES
    masks, narrow_masks = head_masks(F32), head_masks(BF16)
    scale = scale_row(temper_ref, width)

    def window(w, carry):
        rows = pl.ds(pl.multiple_of(w * TOKENS, TOKENS), TOKENS)
        for g in range(groups):
            cols = slice(g * LANES, (g + 1) * LANES)
            d_stack = stack_heads(datt_ref[rows, cols], narrow_masks)
            q_stack = stack_heads(qs_ref[rows, cols], narrow_masks)
            probs = probs_ref[w * groups + g]
            d_probs = mm_nt(v_ref[rows, cols], d_stack)
            wide = probs.astype(F32)
            prod = wide * d_probs
            d_scores = (prod - wide * jnp.sum(prod, axis=0, keepdims=True)).astype(BF16)
            dqkv_ref[rows, slice(2 * width + g * LANES, 2 * width + (g + 1) * LANES)] = mm(
                probs, d_stack
            ).astype(BF16)
            dk_ref[rows, cols] = mm(d_scores, q_stack)
            dq_ref[rows, cols] = unstack_heads(mm_tn(d_scores, kn_ref[rows, cols]), masks)
        return carry

    lax.fori_loop(0, count, window, 0, unroll=True)
    scales = ((scale, 1.0 / (scale * (LOG2_E * LOG2_E))), (1.0 / LOG2_E, 1.0 / LOG2_E))
    for part, (unit_ref, grad_ref) in enumerate(((qs_ref, dq_ref), (kn_ref, dk_ref))):
        cols = slice(part * width, (part + 1) * width)
        unit, grad = unit_ref[...].astype(F32), grad_ref[...]
        along = unit * head_mean(grad * unit)
        first, second = scales[part]
        dqkv_ref[:, cols] = (inv_ref[:, cols] * (grad * first - along * second)).astype(BF16)
    ups = factors(region_ref, up_ref, ups_ref)
    d_qkv = dqkv_ref[...]
    back = (mm_nt(d_qkv, ups) * adapter_columns(tokens, ups.shape[0])).astype(BF16)
    grads_ref[:, :width] = mm_tn(back, normed_ref[...])
    grads_ref[:, width:] = mm_tn(low_ref[...], d_qkv)
    blocks = grads_ref.shape[1] // LANES
    rank = grads_ref.shape[0] // count
    row = lax.broadcasted_iota(jnp.int32, (count, LANES), 0)
    ids = jnp.zeros((count, LANES), F32)
    per = region_ref.shape[2]
    for w in range(count):
        ids = jnp.where(row == w, region_ref[w // per, 0, w % per].astype(F32), ids)
    for b in range(blocks):
        cols = slice(b * LANES, (b + 1) * LANES)
        for r in range(rank):
            own = [grads_ref[w * rank + r : w * rank + r + 1, cols] for w in range(count)]
            tile = jnp.concatenate(own + [ids], axis=0)
            terms_ref[r * blocks + b] = tile.astype(terms_ref.dtype)


def reduce_kernel(terms_ref, sums_ref):
    _, pieces, regions, _ = sums_ref.shape
    devices, _, height, _ = terms_ref.shape
    for p in range(pieces):
        tile = terms_ref[:, p].astype(F32).reshape(devices * height, LANES)
        ids = pltpu.roll(tile, devices * height - height // 2, 0)
        row = lax.broadcasted_iota(jnp.int32, tile.shape, 0) % height
        lane = lax.broadcasted_iota(jnp.int32, tile.shape, 1).astype(F32)
        hot = jnp.where((ids == lane) & (row < height // 2), 1.0, 0.0).astype(BF16)
        sums = mm_tn(hot, tile.astype(BF16))[:regions].astype(sums_ref.dtype)
        for d in range(sums_ref.shape[0]):
            sums_ref[d, p] = sums


def scale_kernel(near_ref, far_ref, down_ref, up_ref, all_ref):
    regions, _, width = down_ref.shape
    rank, blocks = all_ref.shape[:2]
    outer, inner = near_ref.shape[:2]
    core = lax.axis_index("lat") % 2
    total = jnp.zeros((regions, LANES), F32)
    for side, ref in enumerate((near_ref, far_ref)):
        which = core if side == 0 else 1 - core
        for a in range(outer):
            for r in range(inner):
                for b in range(blocks):
                    part = ref[a, r, b].astype(F32)
                    total += part * part
                    all_ref[(a * 2 + which) * inner + r, b] = part
    size = rank * blocks * regions * LANES
    total = jnp.sum(jnp.sum(total, axis=0, keepdims=True), axis=1, keepdims=True)
    factor = lax.rsqrt(total * (1.0 / size) + 1e-06)
    for b in range(blocks):
        part = jnp.swapaxes(all_ref[:, b] * factor, 0, 1)
        start = b * LANES
        if start < width:
            down_ref[:, :, start : start + LANES] = part
        else:
            up_ref[:, :, start - width : start - width + LANES] = part


SMEM = pl.BlockSpec(memory_space=pltpu.SMEM)
VMEM = pl.BlockSpec(memory_space=pltpu.VMEM)


def call(kernel, places, outs, scratch=(), flops=0, moved=0, mib=32, name=None):
    return pl.pallas_call(
        kernel,
        in_specs=places,
        out_shape=outs,
        scratch_shapes=[pltpu.VMEM(dims, dtype) for dims, dtype in scratch],
        compiler_params=pltpu.CompilerParams(vmem_limit_bytes=mib * 1024 * 1024),
        cost_estimate=pl.CostEstimate(flops=flops, bytes_accessed=moved, transcendentals=0),
        name=name,
    )


def shape(*dims, dtype=F32):
    return jax.ShapeDtypeStruct(dims, dtype)


def move(array, step):
    lats, lons = lax.axis_size("lat"), lax.axis_size("lon")

    def index(a, b):
        return (a % lats) * lons + b % lons

    pairs = [
        (index(a, b), index(a + step[0], b + step[1])) for a in range(lats) for b in range(lons)
    ]
    return lax.ppermute(array, ("lat", "lon"), pairs)


def halos(field):
    return (
        field[:, :HALF_LAT, HALF_LON:],
        field[:, HALF_LAT:, :HALF_LON],
        field[:, :HALF_LAT, :HALF_LON],
    )


def move_halos(parts):
    south, east, corner = parts
    corner, east = move(corner, (-1, -1)), move(east, (0, -1))
    return move(south, (-1, 0)), east, corner


def local(
    pixels,
    land_patch_mask,
    region,
    patch_embed_weight,
    patch_embed_bias,
    land_embedding_vector,
    attention_norm_gain,
    query_key_value_weight,
    region_down_factor,
    region_up_factor,
    head_logit_scale,
    attention_output_weight,
    feedforward_gain,
    feedforward_up_weight,
    feedforward_down_weight,
    cotangent,
):
    levels, rows, cols, patch_len = pixels.shape
    width = patch_embed_weight.shape[1]
    inner = feedforward_up_weight.shape[1]
    regions, rank, _ = region_down_factor.shape
    count = region.size
    tokens = count * TOKENS
    groups = width // LANES
    devices = lax.axis_size("lat") * lax.axis_size("lon")

    wide = (levels, HALF_LAT, cols - HALF_LON, width)
    narrow = (levels, HALF_LAT, HALF_LON, width)
    pix_own, *pix = call(
        pack_kernel,
        [VMEM] * 2,
        tuple(shape(*dims, dtype=BF16) for dims in (wide, wide, narrow, narrow)),
        moved=2_000_000,
        name="pack_pixels",
    )(pixels, land_patch_mask.astype(BF16))
    pix, cotangent = lax.optimization_barrier((pix, cotangent))
    pix = move_halos(pix)
    cot_own = cotangent[:, HALF_LAT:, HALF_LON:].astype(BF16)
    cot = move_halos(tuple(part.astype(BF16) for part in halos(cotangent)))

    hidden, normed, low, inv, qs, kn, v, probs = call(
        attention_kernel,
        [SMEM] * 2 + [VMEM] * 12,
        (
            shape(tokens, width),
            shape(tokens, width, dtype=BF16),
            shape(tokens, rank * count, dtype=BF16),
            shape(tokens, 2 * width),
            shape(tokens, width, dtype=BF16),
            shape(tokens, width, dtype=BF16),
            shape(tokens, width, dtype=BF16),
            shape(count * groups, TOKENS, PER_GROUP * TOKENS, dtype=BF16),
        ),
        (
            ((tokens, width), F32),
            ((tokens, width), BF16),
            ((rank * count, width), F32),
            ((rank * count, 3 * width), F32),
            ((levels // WLEV, TOKENS, PER_GROUP * TOKENS), F32),
        ),
        flops=2 * tokens * width * 6 * width,
        moved=20_000_000,
        name="attention_forward",
    )(
        region, head_logit_scale, pix_own, *pix, patch_embed_weight, patch_embed_bias[None],
        land_embedding_vector[None], attention_norm_gain[None], query_key_value_weight,
        region_down_factor, region_up_factor, attention_output_weight,
    )
    home, north, west, diagonal, d_att = call(
        feed_kernel,
        [VMEM] * 9,
        (
            shape(*wide),
            shape(*wide, dtype=BF16),
            shape(*narrow, dtype=BF16),
            shape(*narrow, dtype=BF16),
            shape(tokens, width, dtype=BF16),
        ),
        (((tokens, width), F32),) * 3,
        flops=2 * tokens * width * 4 * inner,
        moved=20_000_000,
        name="feed_forward",
    )(
        hidden, cot_own, *cot, feedforward_gain[None], feedforward_up_weight, feedforward_down_weight,
        attention_output_weight,
    )
    pieces = rank * 4 * width // LANES
    terms = call(
        backward_kernel,
        [SMEM] * 2 + [VMEM] * 9,
        shape(pieces, 2 * count, LANES, dtype=BF16),
        (
            ((tokens, width), F32),
            ((tokens, width), F32),
            ((tokens, 3 * width), BF16),
            ((rank * count, 3 * width), F32),
            ((rank * count, 4 * width), F32),
        ),
        flops=2 * tokens * width * 4 * width,
        moved=12_000_000,
        name="attention_backward",
    )(
        region, head_logit_scale, normed, low, inv, qs, kn, v, probs, d_att, region_up_factor
    )
    each = pieces // devices
    terms = lax.all_to_all(terms, AXES, 0, 0, tiled=True)
    sums = call(
        reduce_kernel,
        [VMEM],
        shape(devices // 2, each, regions, LANES, dtype=BF16),
        name="sum_by_region",
    )(terms.reshape(devices, each, 2 * count, LANES))
    lats, lons = lax.axis_size("lat"), lax.axis_size("lon")
    cores = [[a * lons + b for a in range(c, lats, 2) for b in range(lons)] for c in range(2)]
    near = lax.all_to_all(sums, AXES, 0, 0, axis_index_groups=cores, tiled=True)
    diagonal, west, north = move(diagonal, (1, 1)), move(west, (0, 1)), move(north, (1, 0))
    near, diagonal, west, north = lax.optimization_barrier((near, diagonal, west, north))
    upper = jnp.concatenate((diagonal, north), axis=2).astype(F32)
    lower = jnp.concatenate((west.astype(F32), home), axis=2)
    mixed_state = jnp.concatenate((upper, lower), axis=1)
    far = lax.ppermute(near, "lat", [(a, a ^ 1) for a in range(lats)])
    blocks = 4 * width // LANES
    order = (lats // 2, rank // lats, blocks, regions, LANES)
    step_down, step_up = call(
        scale_kernel,
        [VMEM] * 2,
        (shape(regions, rank, width), shape(regions, rank, 3 * width)),
        (((rank, blocks, regions, LANES), F32),),
        name="scale_steps",
    )(near.reshape(order), far.reshape(order))
    return (mixed_state, step_down, step_up)


def solution(mesh):
    field = P(None, "lat", "lon", None)
    placed = (field, P("lat", "lon"), P(None, "lat", "lon")) + (P(),) * 12 + (field,)
    return jax.shard_map(
        local, mesh=mesh, in_specs=placed, out_specs=(field, P(), P()), check_vma=False
    )
```

```python
import jax
import jax.numpy as jnp
from jax import lax
from jax.experimental import pallas as pl
from jax.experimental.pallas import tpu as pltpu
from jax.sharding import PartitionSpec as P

WLEV = 2
WLAT = 6
WLON = 12
TOKENS = WLEV * WLAT * WLON
HALF_LAT = WLAT // 2
HALF_LON = WLON // 2
LANES = 128
HEAD = 32
PER_GROUP = LANES // HEAD

AXES = ("lat", "lon")
LOG2_E = 1.4426950408889634
F32 = jnp.float32
BF16 = jnp.bfloat16


def mm(a, b):
    return lax.dot_general(a, b, (((1,), (0,)), ((), ())), preferred_element_type=F32)


def mm_nt(a, b):
    return lax.dot_general(a, b, (((1,), (1,)), ((), ())), preferred_element_type=F32)


def mm_tn(a, b):
    return lax.dot_general(a, b, (((0,), (0,)), ((), ())), preferred_element_type=F32)


def head_mean(values, exact=True):
    wide = 2 * LANES
    rows = lax.broadcasted_iota(jnp.int32, (wide, wide), 0) // HEAD
    cols = lax.broadcasted_iota(jnp.int32, (wide, wide), 1) // HEAD
    block = jnp.where(rows == cols, 1.0 / HEAD, 0.0).astype(BF16)
    parts = []
    for start in range(0, values.shape[1], wide):
        part = values[:, start : start + wide]
        top = part.astype(BF16)
        mean = mm(top, block)
        if exact:
            mean += mm((part - top.astype(F32)).astype(BF16), block)
        parts.append(mean)
    return jnp.concatenate(parts, axis=1)


def head_masks(dtype):
    lane = lax.broadcasted_iota(jnp.int32, (1, LANES), 1) // HEAD
    return [jnp.where(lane == h, 1.0, 0.0).astype(dtype) for h in range(PER_GROUP)]


def stack_heads(x, masks):
    return jnp.concatenate([x * m for m in masks], axis=0)


def unstack_heads(x, masks):
    tokens = x.shape[0] // PER_GROUP
    return sum(x[h * tokens : (h + 1) * tokens] * m for h, m in enumerate(masks))


def adapter_columns(tokens, columns):
    rank = columns // (tokens // TOKENS)
    own = lax.broadcasted_iota(jnp.int32, (tokens, columns), 0)
    first = lax.broadcasted_iota(jnp.int32, (tokens, columns), 1) // rank * TOKENS
    return jnp.where((own >= first) & (own < first + TOKENS), 1.0, 0.0)


def factors(region_ref, factor_ref, all_ref):
    rank = factor_ref.shape[1]
    ids = [region_ref[a, 0, b] for a in range(region_ref.shape[0]) for b in range(region_ref.shape[2])]
    for w, r in enumerate(ids):
        all_ref[w * rank : (w + 1) * rank, :] = factor_ref[r].astype(F32)
    return all_ref[...].astype(BF16)


def scale_row(scale_ref, width):
    head = lax.broadcasted_iota(jnp.int32, (1, width), 1) // HEAD
    row = jnp.zeros((1, width), F32)
    for h in range(width // HEAD):
        row = jnp.where(head == h, scale_ref[h] / HEAD, row)
    return row


def same_group(level, south):
    def group(token):
        late = jnp.where(token >= TOKENS // WLEV, 1, 0) * level
        low = jnp.where(token // WLON % WLAT >= HALF_LAT, 1, 0) * south
        return 2 * late + low

    keys = lax.broadcasted_iota(jnp.int32, (TOKENS, 1), 0)
    queries = lax.broadcasted_iota(jnp.int32, (1, PER_GROUP * TOKENS), 1) % TOKENS
    return jnp.where(group(keys) == group(queries), 1.0, 0.0)


def pieces_of(shape):
    levels, _, cols, _ = shape
    across = (cols + HALF_LON) // WLON
    for level in range(levels):
        for row in range(WLAT):
            within = level % WLEV * WLAT * WLON + row * WLON
            starts = [((level // WLEV) * across + b) * TOKENS + within for b in range(across)]
            yield (level + WLEV // 2) % levels, row // HALF_LAT, row % HALF_LAT, starts


def into_windows(stage_ref, own_ref, south_ref, east_ref, corner_ref):
    for level, half, row, starts in pieces_of(own_ref.shape):
        wide = (south_ref if half else own_ref)[level, row].astype(F32)
        narrow = (corner_ref if half else east_ref)[level, row].astype(F32)
        for b, start in enumerate(starts[:-1]):
            stage_ref[start : start + WLON, :] = wide[b * WLON : (b + 1) * WLON]
        start = starts[-1]
        stage_ref[start : start + HALF_LON, :] = wide[-HALF_LON:]
        stage_ref[start + HALF_LON : start + WLON, :] = narrow


def out_of_windows(stage_ref, own_ref, north_ref, west_ref, corner_ref):
    for level, half, row, starts in pieces_of(own_ref.shape):
        wide = [stage_ref[start : start + WLON, :] for start in starts[:-1]]
        start = starts[-1]
        wide.append(stage_ref[start : start + HALF_LON, :])
        narrow = stage_ref[start + HALF_LON : start + WLON, :]
        wide_ref, narrow_ref = (north_ref, corner_ref) if half else (own_ref, west_ref)
        wide_ref[level, row] = jnp.concatenate(wide, axis=0).astype(wide_ref.dtype)
        narrow_ref[level, row] = narrow.astype(narrow_ref.dtype)


def norm_stats(x):
    width = x.shape[1]
    mean = jnp.sum(x, axis=1, keepdims=True) * (1.0 / width)
    centred = x - mean
    spread = jnp.sum(centred * centred, axis=1, keepdims=True) * (1.0 / width)
    return centred, lax.rsqrt(spread + 1e-05)


def gelu_and_slope(u):
    phi = 0.5 + 0.5 * lax.erf(u * 0.5**0.5)
    return u * phi, phi + (0.3989422804014327 * u) * jnp.exp2((-0.5 * LOG2_E) * (u * u))


def pack_kernel(pixels_ref, land_ref, own_ref, south_ref, east_ref, corner_ref):
    levels, rows, cols, patch_len = pixels_ref.shape
    width = own_ref.shape[3]
    eye = lax.broadcasted_iota(jnp.int32, (cols, cols), 0)
    eye = jnp.where(eye == lax.broadcasted_iota(jnp.int32, (cols, cols), 1), 1.0, 0.0)
    land = mm_nt(eye.astype(BF16), land_ref[...])
    lane = lax.broadcasted_iota(jnp.int32, (cols, width), 1)
    blank = jnp.zeros((cols, width - patch_len), F32)
    for level in range(levels):
        for row in range(rows):
            patch = jnp.concatenate((pixels_ref[level, row].astype(F32), blank), axis=1)
            patch = jnp.where(lane == patch_len, land[:, row : row + 1], patch).astype(BF16)
            half, at = divmod(row, HALF_LAT)
            (own_ref if half else south_ref)[level, at] = patch[HALF_LON:]
            (east_ref if half else corner_ref)[level, at] = patch[:HALF_LON]


def attention_kernel(
    region_ref, temper_ref, own_ref, south_ref, east_ref, corner_ref, wp_ref, bias_ref, land_ref,
    gain_ref, wqkv_ref, down_ref, up_ref, wo_ref,
    hidden_ref, normed_ref, low_ref, inv_ref, qs_ref, kn_ref, v_ref, probs_ref,
    state_ref, att_ref, downs_ref, ups_ref, same_ref,
):
    tokens, width = state_ref.shape
    count = tokens // TOKENS
    groups = width // LANES
    masks, narrow_masks = head_masks(F32), head_masks(BF16)
    patch_len = wp_ref.shape[0]
    into_windows(state_ref, own_ref, south_ref, east_ref, corner_ref)
    pix = state_ref[:, :patch_len].astype(BF16)
    land = state_ref[:, patch_len : patch_len + 1]
    state = mm(pix, wp_ref[...]) + bias_ref[...] + land * land_ref[...]
    state_ref[...] = state
    centred, inv = norm_stats(state)
    normed = (centred * inv * gain_ref[...]).astype(BF16)
    normed_ref[...] = normed
    downs = factors(region_ref, down_ref, downs_ref)
    ups = factors(region_ref, up_ref, ups_ref)
    low = (mm_nt(normed, downs) * adapter_columns(tokens, downs.shape[0])).astype(BF16)
    low_ref[...] = low
    scale = scale_row(temper_ref, width)
    for part in range(3):
        cols = slice(part * width, (part + 1) * width)
        qkv = mm(normed, wqkv_ref[:, cols]) + mm(low, ups[:, cols])
        if part == 2:
            v_ref[...] = qkv.astype(BF16)
        else:
            inv = lax.rsqrt(head_mean(qkv * qkv) + 1e-06)
            inv_ref[:, cols] = inv
            if part == 0:
                qs_ref[...] = (qkv * inv * (scale * LOG2_E)).astype(BF16)
            else:
                kn_ref[...] = (qkv * inv).astype(BF16)
    last_band = lax.axis_index("lat") == lax.axis_size("lat") - 1
    south = jnp.where(last_band, 1, 0).astype(jnp.int32)
    parts = same_ref.shape[0]
    for part in range(parts):
        same_ref[part] = same_group(1 if part == parts - 1 else 0, south)

    def window(w, carry):
        rows = pl.ds(pl.multiple_of(w * TOKENS, TOKENS), TOKENS)
        same = same_ref[w // (count // parts)]
        for g in range(groups):
            cols = slice(g * LANES, (g + 1) * LANES)
            stack = stack_heads(qs_ref[rows, cols], narrow_masks)
            weights = jnp.exp2(mm_nt(kn_ref[rows, cols], stack)) * same
            total = jnp.sum(weights, axis=0, keepdims=True)
            probs = (weights * (1.0 / total)).astype(BF16)
            probs_ref[w * groups + g] = probs
            mixed = mm_tn(probs, v_ref[rows, cols])
            att_ref[rows, cols] = unstack_heads(mixed, masks).astype(BF16)
        return carry

    lax.fori_loop(0, count, window, 0, unroll=True)
    z = mm(att_ref[...], wo_ref[...]).astype(BF16)
    hidden_ref[...] = state_ref[...] + z.astype(F32)


def feed_kernel(
    hidden_ref, own_ref, south_ref, east_ref, corner_ref, gain_ref, wup_ref, wdn_ref, wo_ref,
    home_ref, north_ref, west_ref, diagonal_ref, datt_ref,
    cot_ref, mixed_ref, unit_ref,
):
    tokens, width = hidden_ref.shape
    into_windows(cot_ref, own_ref, south_ref, east_ref, corner_ref)
    hidden = hidden_ref[...]
    centred, inv = norm_stats(hidden)
    unit = centred * inv
    normed = (unit * gain_ref[...]).astype(BF16)
    cot = cot_ref[...].astype(BF16)
    mixed_ref[...] = hidden
    unit_ref[...] = unit
    d_normed = jnp.zeros((tokens, width), F32)
    chunk = 1024
    for c in range(wup_ref.shape[1] // chunk):
        cols = slice(c * chunk, (c + 1) * chunk)
        act, slope = gelu_and_slope(mm(normed, wup_ref[:, cols]))
        mixed_ref[...] += mm(act.astype(BF16), wdn_ref[cols, :])
        d_up = mm_nt(cot, wdn_ref[cols, :]) * slope
        d_normed += mm_nt(d_up.astype(BF16), wup_ref[:, cols])
    out_of_windows(mixed_ref, home_ref, north_ref, west_ref, diagonal_ref)
    d_unit = d_normed * gain_ref[...]
    unit = unit_ref[...]
    first = jnp.sum(d_unit, axis=1, keepdims=True) * (1.0 / width)
    second = jnp.sum(d_unit * unit, axis=1, keepdims=True) * (1.0 / width)
    d_hidden = cot_ref[...] + inv * (d_unit - first - unit * second)
    datt_ref[...] = mm_nt(d_hidden.astype(BF16), wo_ref[...]).astype(BF16)


def backward_kernel(
    region_ref, temper_ref, normed_ref, low_ref, inv_ref, qs_ref, kn_ref, v_ref, probs_ref, datt_ref,
    up_ref,
    terms_ref,
    dq_ref, dk_ref, dqkv_ref, ups_ref, grads_ref,
):
    tokens, width = normed_ref.shape
    count = tokens // TOKENS
    groups = width // LANES
    masks, narrow_masks = head_masks(F32), head_masks(BF16)
    scale = scale_row(temper_ref, width)

    def window(w, carry):
        rows = pl.ds(pl.multiple_of(w * TOKENS, TOKENS), TOKENS)
        for g in range(groups):
            cols = slice(g * LANES, (g + 1) * LANES)
            d_stack = stack_heads(datt_ref[rows, cols], narrow_masks)
            q_stack = stack_heads(qs_ref[rows, cols], narrow_masks)
            probs = probs_ref[w * groups + g]
            d_probs = mm_nt(v_ref[rows, cols], d_stack)
            wide = probs.astype(F32)
            prod = wide * d_probs
            d_scores = (prod - wide * jnp.sum(prod, axis=0, keepdims=True)).astype(BF16)
            dqkv_ref[rows, slice(2 * width + g * LANES, 2 * width + (g + 1) * LANES)] = mm(
                probs, d_stack
            ).astype(BF16)
            dk_ref[rows, cols] = mm(d_scores, q_stack)
            dq_ref[rows, cols] = unstack_heads(mm_tn(d_scores, kn_ref[rows, cols]), masks)
        return carry

    lax.fori_loop(0, count, window, 0, unroll=True)
    scales = ((scale, 1.0 / (scale * (LOG2_E * LOG2_E))), (1.0 / LOG2_E, 1.0 / LOG2_E))
    for part, (unit_ref, grad_ref) in enumerate(((qs_ref, dq_ref), (kn_ref, dk_ref))):
        cols = slice(part * width, (part + 1) * width)
        unit, grad = unit_ref[...].astype(F32), grad_ref[...]
        along = unit * head_mean(grad * unit, exact=False)
        first, second = scales[part]
        dqkv_ref[:, cols] = (inv_ref[:, cols] * (grad * first - along * second)).astype(BF16)
    ups = factors(region_ref, up_ref, ups_ref)
    d_qkv = dqkv_ref[...]
    back = (mm_nt(d_qkv, ups) * adapter_columns(tokens, ups.shape[0])).astype(BF16)
    grads_ref[:, :width] = mm_tn(back, normed_ref[...])
    grads_ref[:, width:] = mm_tn(low_ref[...], d_qkv)
    blocks = grads_ref.shape[1] // LANES
    rank = grads_ref.shape[0] // count
    row = lax.broadcasted_iota(jnp.int32, (count, LANES), 0)
    ids = jnp.zeros((count, LANES), F32)
    per = region_ref.shape[2]
    for w in range(count):
        ids = jnp.where(row == w, region_ref[w // per, 0, w % per].astype(F32), ids)
    for b in range(blocks):
        cols = slice(b * LANES, (b + 1) * LANES)
        for r in range(rank):
            own = [grads_ref[w * rank + r : w * rank + r + 1, cols] for w in range(count)]
            tile = jnp.concatenate(own + [ids], axis=0)
            terms_ref[r * blocks + b] = tile.astype(terms_ref.dtype)


def reduce_kernel(terms_ref, sums_ref):
    _, pieces, regions, _ = sums_ref.shape
    devices, _, height, _ = terms_ref.shape
    for p in range(pieces):
        tile = terms_ref[:, p].astype(F32).reshape(devices * height, LANES)
        ids = pltpu.roll(tile, devices * height - height // 2, 0)
        row = lax.broadcasted_iota(jnp.int32, tile.shape, 0) % height
        lane = lax.broadcasted_iota(jnp.int32, tile.shape, 1).astype(F32)
        hot = jnp.where((ids == lane) & (row < height // 2), 1.0, 0.0).astype(BF16)
        sums = mm_tn(hot, tile.astype(BF16))[:regions].astype(sums_ref.dtype)
        for d in range(sums_ref.shape[0]):
            sums_ref[d, p] = sums


def scale_kernel(near_ref, far_ref, down_ref, up_ref, all_ref):
    regions, _, width = down_ref.shape
    rank, blocks = all_ref.shape[:2]
    outer, inner = near_ref.shape[:2]
    core = lax.axis_index("lat") % 2
    total = jnp.zeros((regions, LANES), F32)
    for side, ref in enumerate((near_ref, far_ref)):
        which = core if side == 0 else 1 - core
        for a in range(outer):
            for r in range(inner):
                for b in range(blocks):
                    part = ref[a, r, b].astype(F32)
                    total += part * part
                    all_ref[(a * 2 + which) * inner + r, b] = part
    size = rank * blocks * regions * LANES
    total = jnp.sum(jnp.sum(total, axis=0, keepdims=True), axis=1, keepdims=True)
    factor = lax.rsqrt(total * (1.0 / size) + 1e-06)
    for b in range(blocks):
        part = jnp.swapaxes(all_ref[:, b] * factor, 0, 1)
        start = b * LANES
        if start < width:
            down_ref[:, :, start : start + LANES] = part
        else:
            up_ref[:, :, start - width : start - width + LANES] = part


SMEM = pl.BlockSpec(memory_space=pltpu.SMEM)
VMEM = pl.BlockSpec(memory_space=pltpu.VMEM)


def call(kernel, places, outs, scratch=(), flops=0, moved=0, mib=32, name=None):
    return pl.pallas_call(
        kernel,
        in_specs=places,
        out_shape=outs,
        scratch_shapes=[pltpu.VMEM(dims, dtype) for dims, dtype in scratch],
        compiler_params=pltpu.CompilerParams(vmem_limit_bytes=mib * 1024 * 1024),
        cost_estimate=pl.CostEstimate(flops=flops, bytes_accessed=moved, transcendentals=0),
        name=name,
    )


def shape(*dims, dtype=F32):
    return jax.ShapeDtypeStruct(dims, dtype)


def move(array, step):
    lats, lons = lax.axis_size("lat"), lax.axis_size("lon")

    def index(a, b):
        return (a % lats) * lons + b % lons

    pairs = [
        (index(a, b), index(a + step[0], b + step[1])) for a in range(lats) for b in range(lons)
    ]
    return lax.ppermute(array, ("lat", "lon"), pairs)


def halos(field):
    return (
        field[:, :HALF_LAT, HALF_LON:],
        field[:, HALF_LAT:, :HALF_LON],
        field[:, :HALF_LAT, :HALF_LON],
    )


def move_halos(parts):
    south, east, corner = parts
    corner, east = move(corner, (-1, -1)), move(east, (0, -1))
    return move(south, (-1, 0)), east, corner


def local(
    pixels,
    land_patch_mask,
    region,
    patch_embed_weight,
    patch_embed_bias,
    land_embedding_vector,
    attention_norm_gain,
    query_key_value_weight,
    region_down_factor,
    region_up_factor,
    head_logit_scale,
    attention_output_weight,
    feedforward_gain,
    feedforward_up_weight,
    feedforward_down_weight,
    cotangent,
):
    levels, rows, cols, patch_len = pixels.shape
    width = patch_embed_weight.shape[1]
    inner = feedforward_up_weight.shape[1]
    regions, rank, _ = region_down_factor.shape
    count = region.size
    tokens = count * TOKENS
    groups = width // LANES
    devices = lax.axis_size("lat") * lax.axis_size("lon")

    wide = (levels, HALF_LAT, cols - HALF_LON, width)
    narrow = (levels, HALF_LAT, HALF_LON, width)
    pix_own, *pix = call(
        pack_kernel,
        [VMEM] * 2,
        tuple(shape(*dims, dtype=BF16) for dims in (wide, wide, narrow, narrow)),
        moved=2_000_000,
        name="pack_pixels",
    )(pixels, land_patch_mask.astype(BF16))
    pix, cotangent = lax.optimization_barrier((pix, cotangent))
    pix = move_halos(pix)
    cot_own = cotangent[:, HALF_LAT:, HALF_LON:].astype(BF16)
    cot = move_halos(tuple(part.astype(BF16) for part in halos(cotangent)))

    hidden, normed, low, inv, qs, kn, v, probs = call(
        attention_kernel,
        [SMEM] * 2 + [VMEM] * 12,
        (
            shape(tokens, width),
            shape(tokens, width, dtype=BF16),
            shape(tokens, rank * count, dtype=BF16),
            shape(tokens, 2 * width),
            shape(tokens, width, dtype=BF16),
            shape(tokens, width, dtype=BF16),
            shape(tokens, width, dtype=BF16),
            shape(count * groups, TOKENS, PER_GROUP * TOKENS, dtype=BF16),
        ),
        (
            ((tokens, width), F32),
            ((tokens, width), BF16),
            ((rank * count, width), F32),
            ((rank * count, 3 * width), F32),
            ((levels // WLEV, TOKENS, PER_GROUP * TOKENS), F32),
        ),
        flops=2 * tokens * width * 6 * width,
        moved=20_000_000,
        name="attention_forward",
    )(
        region, head_logit_scale, pix_own, *pix, patch_embed_weight, patch_embed_bias[None],
        land_embedding_vector[None], attention_norm_gain[None], query_key_value_weight,
        region_down_factor, region_up_factor, attention_output_weight,
    )
    home, north, west, diagonal, d_att = call(
        feed_kernel,
        [VMEM] * 9,
        (
            shape(*wide),
            shape(*wide, dtype=BF16),
            shape(*narrow, dtype=BF16),
            shape(*narrow, dtype=BF16),
            shape(tokens, width, dtype=BF16),
        ),
        (((tokens, width), F32),) * 3,
        flops=2 * tokens * width * 4 * inner,
        moved=20_000_000,
        name="feed_forward",
    )(
        hidden, cot_own, *cot, feedforward_gain[None], feedforward_up_weight, feedforward_down_weight,
        attention_output_weight,
    )
    pieces = rank * 4 * width // LANES
    terms = call(
        backward_kernel,
        [SMEM] * 2 + [VMEM] * 9,
        shape(pieces, 2 * count, LANES, dtype=BF16),
        (
            ((tokens, width), F32),
            ((tokens, width), F32),
            ((tokens, 3 * width), BF16),
            ((rank * count, 3 * width), F32),
            ((rank * count, 4 * width), F32),
        ),
        flops=2 * tokens * width * 4 * width,
        moved=12_000_000,
        name="attention_backward",
    )(
        region, head_logit_scale, normed, low, inv, qs, kn, v, probs, d_att, region_up_factor
    )
    each = pieces // devices
    terms = lax.all_to_all(terms, AXES, 0, 0, tiled=True)
    sums = call(
        reduce_kernel,
        [VMEM],
        shape(devices // 2, each, regions, LANES, dtype=BF16),
        name="sum_by_region",
    )(terms.reshape(devices, each, 2 * count, LANES))
    lats, lons = lax.axis_size("lat"), lax.axis_size("lon")
    cores = [[a * lons + b for a in range(c, lats, 2) for b in range(lons)] for c in range(2)]
    near = lax.all_to_all(sums, AXES, 0, 0, axis_index_groups=cores, tiled=True)
    diagonal, west, north = move(diagonal, (1, 1)), move(west, (0, 1)), move(north, (1, 0))
    near, diagonal, west, north = lax.optimization_barrier((near, diagonal, west, north))
    upper = jnp.concatenate((diagonal, north), axis=2).astype(F32)
    lower = jnp.concatenate((west.astype(F32), home), axis=2)
    mixed_state = jnp.concatenate((upper, lower), axis=1)
    far = lax.ppermute(near, "lat", [(a, a ^ 1) for a in range(lats)])
    blocks = 4 * width // LANES
    order = (lats // 2, rank // lats, blocks, regions, LANES)
    step_down, step_up = call(
        scale_kernel,
        [VMEM] * 2,
        (shape(regions, rank, width), shape(regions, rank, 3 * width)),
        (((rank, blocks, regions, LANES), F32),),
        name="scale_steps",
    )(near.reshape(order), far.reshape(order))
    return (mixed_state, step_down, step_up)


def solution(mesh):
    field = P(None, "lat", "lon", None)
    placed = (field, P("lat", "lon"), P(None, "lat", "lon")) + (P(),) * 12 + (field,)
    return jax.shard_map(
        local, mesh=mesh, in_specs=placed, out_specs=(field, P(), P()), check_vma=False
    )
```
